32 devices in a mesh: dp: 2 (over core), row: 4 (over z), col: 4 (over y, x).
Axes of the slice: x: 2, y: 2, z: 4, core: 2. Of those that a mesh axis runs over, the one named last changes fastest.
Arguments:
- tokens: bfloat16 [16384, 1024], P(('dp', 'row', 'col')), may hold values from -6 to 6
- segment_ids: int32 [16, 1024], P(('dp', 'row')), may hold values from 0 to 2, never falling along the last dimension, each value on 1 to 512 neighbouring positions
- in_weight: bfloat16 [1024, 3072], P('row', 'col'), may hold values from -0.1875 to 0.1875
- in_bias: float32 [2048], P('col'), may hold values from -3 to 3
- out_weight: bfloat16 [1024, 1024], P('col', 'row'), may hold values from -3 to 3
- out_bias: float32 [1024], replicated, may hold values from -3 to 3
- gain_one: float32 [1024], replicated, may hold values from 0.25 to 1.75
- shift_one: float32 [1024], replicated, may hold values from -3 to 3
- up_weight: bfloat16 [1024, 4096], P('row', 'col'), may hold values from -0.1875 to 0.1875
- up_bias: float32 [4096], P('col'), may hold values from -3 to 3
- down_weight: bfloat16 [4096, 1024], P('col', 'row'), may hold values from -0.09375 to 0.09375
- down_bias: float32 [1024], replicated, may hold values from -3 to 3
- gain_two: float32 [1024], replicated, may hold values from 0.25 to 1.75
- shift_two: float32 [1024], replicated, may hold values from -3 to 3
- cotangent: bfloat16 [16384, 1024], P(('dp', 'row', 'col')), may hold values from -6 to 6
Outputs:
- output: bfloat16 [16384, 1024], P(('dp', 'row', 'col'))
- grad_tokens: float32 [16384, 1024], P(('dp', 'row', 'col'))
- grad_in_weight: float32 [1024, 3072], P('row', 'col')
- grad_in_bias: float32 [2048], P('col')
- grad_out_weight: float32 [1024, 1024], P('col', 'row')
- grad_out_bias: float32 [1024], replicated
- grad_gain_one: float32 [1024], replicated
- grad_shift_one: float32 [1024], replicated
- grad_up_weight: float32 [1024, 4096], P('row', 'col')
- grad_up_bias: float32 [4096], P('col')
- grad_down_weight: float32 [4096, 1024], P('col', 'row')
- grad_down_bias: float32 [1024], replicated
- grad_gain_two: float32 [1024], replicated
- grad_shift_two: float32 [1024], replicated
The draws below stay inside these ranges and needn't reach their ends.
Inputs may be any that keep to these rules, and one draw needn't show every extreme that they name: `segment_ids`: along each sequence the ids never fall; each sequence holds 3 documents of 1 to 512 tokens, one of exactly 512.
All inputs are finite; a program needn't handle non-finite values.
Results may differ from the reference program's by a relative error of at most 0.02.
Values may be sent and summed in bfloat16 or wider, within the bound.
No kernel may reach another device: no remote copies, remote signals or barrier semaphores. Data moves between devices by JAX's collectives and lax.ppermute only.
A program may use at most 128 MiB of HBM per device.

```python
import math
import jax
import jax.numpy as jnp
import numpy as np
from jax import lax

D = 1024
HEADS = 16
HD = 64
FF = 4096
LEN = 1024
SEGS = 3
MOST_DOC = 512
NSEQ = 16
TOKENS = 16384


def levels(key, extent, shards, smallest, high):
    loudness = 1.0
    for dim, blocks in shards:
        steps = jax.random.uniform(jax.random.fold_in(jax.random.fold_in(key, 6), dim), (blocks,), jnp.float32, smallest / len(shards), high / len(shards))
        loudness = loudness * jnp.repeat(jnp.exp(steps), extent[dim] // blocks).reshape((-1,) + (1,) * (len(extent) - 1 - dim))
    return loudness


def profile(count, total, limit, skew):
    loads = [(1 << 20) // math.isqrt(grade ** skew) + 1 for grade in range(2, count + 1)]
    rest, given = total - limit - (count - 1), [1] * (count - 1)
    while rest > 0:
        movable = [i for i in range(count - 1) if given[i] < limit]
        mass, remaining = sum([loads[i] for i in movable]), rest
        for i in movable:
            addition = min(limit - given[i], max(1, remaining * loads[i] // mass), rest)
            given[i] = given[i] + addition
            rest = rest - addition
    return np.array([limit] + given)


def ragged(rng, amount, total, limit, skew):
    if amount == 2:
        one = jax.random.randint(rng, (), max(1, total - limit), min(limit, total - 1) + 1)
        return jnp.stack([one, total - one])
    lengths = jnp.asarray(profile(amount, total, limit, skew), jnp.int32)
    twos = (amount - 1) // 2
    giver, receiver = lengths[1:1 + 2 * twos:2], lengths[2:2 + 2 * twos:2]
    slack = jnp.minimum(giver - 1, limit - receiver)
    shifted = jax.random.randint(jax.random.fold_in(rng, 1), (twos,), 0, 1 << 20) % (slack + 1)
    lengths = lengths.at[1:1 + 2 * twos:2].set(giver - shifted).at[2:2 + 2 * twos:2].set(receiver + shifted)
    return lengths[jax.random.permutation(jax.random.fold_in(rng, 2), amount)]


def centred(stream_key, extent, deviation, limit, shards=(), held_as=jnp.bfloat16):
    drawn = jax.random.normal(stream_key, extent, jnp.float32) * deviation
    if len(shards) > 0:
        drawn = levels(stream_key, extent, shards, -0.22, 0.18) * drawn
    return jnp.clip(drawn, min=-limit, max=limit).astype(held_as)


def setup_inputs(seed: int = 0) -> dict:
    arg_keys = jax.random.split(jax.random.key(seed), 16)
    tokens = centred(arg_keys[0], (TOKENS, D), 1.0, 6.0, ((0, 32),))
    segment_ids = jax.vmap(lambda own: jnp.searchsorted(jnp.cumsum(ragged(own, SEGS, LEN, MOST_DOC, 2)), jnp.arange(LEN), side="right"))(jax.random.split(arg_keys[1], NSEQ)).reshape((NSEQ, LEN)).astype(jnp.int32)
    in_weight = centred(arg_keys[2], (D, 3 * D), D ** -0.5, 0.1875, ((0, 4), (1, 4)))
    in_bias = centred(arg_keys[3], (2 * D,), 0.5, 3.0, ((0, 4),), jnp.float32)
    out_weight = centred(arg_keys[4], (D, D), (max(D // 256, 1)) ** -0.5, 3.0, ((0, 4), (1, 4)))
    out_bias = centred(arg_keys[5], (D,), 0.5, 3.0, (), jnp.float32)
    gain_one = jnp.clip(1.0 + 0.15 * jax.random.normal(arg_keys[6], (D,), jnp.float32), 0.25, 1.75)
    shift_one = centred(arg_keys[7], (D,), 0.5, 3.0, (), jnp.float32)
    up_weight = centred(arg_keys[8], (D, FF), D ** -0.5, 0.1875, ((0, 4), (1, 4)))
    up_bias = centred(arg_keys[9], (FF,), 0.5, 3.0, ((0, 4),), jnp.float32)
    down_weight = centred(arg_keys[10], (FF, D), FF ** -0.5, 0.09375, ((0, 4), (1, 4)))
    down_bias = centred(arg_keys[11], (D,), 0.5, 3.0, (), jnp.float32)
    gain_two = jnp.clip(1.0 + 0.15 * jax.random.normal(arg_keys[12], (D,), jnp.float32), 0.25, 1.75)
    shift_two = centred(arg_keys[13], (D,), 0.5, 3.0, (), jnp.float32)
    cotangent = centred(arg_keys[14], (TOKENS, D), 1.0, 6.0, ((0, 32),))
    return {"tokens": tokens, "segment_ids": segment_ids, "in_weight": in_weight, "in_bias": in_bias, "out_weight": out_weight, "out_bias": out_bias, "gain_one": gain_one, "shift_one": shift_one, "up_weight": up_weight, "up_bias": up_bias, "down_weight": down_weight, "down_bias": down_bias, "gain_two": gain_two, "shift_two": shift_two, "cotangent": cotangent}


NORM_EPSILON = 1e-12
PRECISE = lax.Precision.HIGHEST

@jax.custom_vjp
def low(v):
    return lax.optimization_barrier(v.astype(jnp.bfloat16)).astype(jnp.float32)

@jax.custom_vjp
def low_back(v):
    return v

def low_keep(v):
    return (low(v), None)

def low_pass(kept, grad):
    return (grad,)

def back_keep(v):
    return (v, None)

def back_low(kept, grad):
    return (low(grad),)
low.defvjp(low_keep, low_pass)
low_back.defvjp(back_keep, back_low)

def product(left, right):
    return jnp.dot(left, right, precision=PRECISE, preferred_element_type=jnp.float32)

def layer_norm(hidden, gain, shift):
    row_mean = lax.optimization_barrier(jnp.mean(hidden, axis=1, keepdims=True))
    variance = lax.optimization_barrier(jnp.mean(hidden * hidden, axis=1, keepdims=True)) - row_mean * row_mean
    return (hidden - row_mean) * lax.rsqrt(variance + NORM_EPSILON) * gain + shift

def attend(packed):
    queries, key_rows, value_rows, doc_ids = packed
    scores = jnp.einsum('qhe,khe->hqk', queries, key_rows, precision=PRECISE) * HD ** (-0.5)
    scores = low_back(scores)
    same_doc = doc_ids[:, None] == doc_ids[None, :]
    scores = jnp.where(same_doc[None], scores, -1000000000.0)
    row_top = lax.optimization_barrier(jnp.max(scores, axis=2, keepdims=True))
    exp_terms = jnp.exp(scores - row_top)
    attn_probs = exp_terms / lax.optimization_barrier(jnp.sum(exp_terms, axis=2, keepdims=True))
    return jnp.einsum('hqk,khe->qhe', low(attn_probs), value_rows, precision=PRECISE)

def forward(token_values, doc_ids, in_weight, in_bias, out_weight, out_bias, gain_one, shift_one, up_weight, up_bias, down_weight, down_bias, gain_two, shift_two):
    row_count = token_values.shape[0]
    projected = product(token_values, in_weight).reshape(row_count, HEADS, 3, HD)
    bias_rows = in_bias.reshape(HEADS, 2, HD)
    no_bias = jnp.zeros((HEADS, 1, HD), jnp.float32)
    projected = projected + jnp.concatenate([bias_rows[:, :1], no_bias, bias_rows[:, 1:]], axis=1)
    projected = low(low_back(projected)).reshape(NSEQ, LEN, HEADS, 3, HD)
    attended = lax.map(jax.checkpoint(attend), (projected[:, :, :, 0], projected[:, :, :, 1], projected[:, :, :, 2], doc_ids))
    attended = low(low_back(attended.reshape(row_count, D)))
    residual_one = token_values + low_back(product(attended, out_weight) + out_bias)
    normed_one = layer_norm(residual_one, gain_one, shift_one)
    hidden_pre = low_back(product(low(normed_one), up_weight) + up_bias)
    hidden = low(jax.nn.gelu(hidden_pre, approximate=False))
    residual_two = normed_one + low_back(product(hidden, down_weight) + down_bias)
    return layer_norm(residual_two, gain_two, shift_two)

def reference(tokens, segment_ids, in_weight, in_bias, out_weight, out_bias, gain_one, shift_one, up_weight, up_bias, down_weight, down_bias, gain_two, shift_two, cotangent):
    weights = tuple((array_in.astype(jnp.float32) for array_in in (in_weight, in_bias, out_weight, out_bias, gain_one, shift_one, up_weight, up_bias, down_weight, down_bias, gain_two, shift_two)))

    def run(token_values, *params):
        return forward(token_values, segment_ids, *params)
    output, pullback = jax.vjp(run, tokens.astype(jnp.float32), *weights)
    grads = pullback(cotangent.astype(jnp.float32))
    return (output.astype(jnp.bfloat16), grads[0], grads[1], grads[2], grads[3], grads[4], grads[5], grads[6], grads[7], grads[8], grads[9], grads[10], grads[11], grads[12])
```

```python
from functools import partial
import math

import jax
import jax.numpy as jnp
from jax import lax
from jax.experimental import pallas as pl
from jax.experimental.pallas import tpu as pltpu
from jax.sharding import PartitionSpec as P

HD = 64
NORM_EPSILON = 1e-12
ALL = ("dp", "row", "col")
BF = jnp.bfloat16
F32 = jnp.float32
HIDDEN_SCORE = -1e30
SCALE = HD ** (-0.5)
EXP2_SCALE = SCALE * math.log2(math.e)


class Grid:
    def __init__(self, dp, row, outer, inner):
        self.shape = (dp, row, outer, inner)

    def pairs(self, target):
        n_d, n_r, n_o, n_i = self.shape

        def flat(d, r, o, i):
            return ((d * n_r + r) * n_o + o) * n_i + i

        result = []
        for d in range(n_d):
            for r in range(n_r):
                for o in range(n_o):
                    for i in range(n_i):
                        there = target(d, r, o, i)
                        if there is not None:
                            result.append((flat(d, r, o, i), flat(*there)))
        return result

    def shift(self, value, axis, by):
        size = self.shape[axis]

        def target(*at):
            at = list(at)
            at[axis] = (at[axis] + by) % size
            return tuple(at)

        return lax.ppermute(value, ALL, self.pairs(target))

    def flip(self, value, axis, bit):
        def target(*at):
            at = list(at)
            at[axis] = at[axis] ^ bit
            return tuple(at)

        return lax.ppermute(value, ALL, self.pairs(target))

    def total(self, value):
        for axis, size in enumerate(self.shape):
            bit = 1
            while bit < size:
                value = value + self.flip(value, axis, bit)
                bit *= 2
        return value

    def send_home(self, value):
        def target(d, r, o, i):
            return None if o == d else (d, r, d, i)

        return lax.ppermute(value, ALL, self.pairs(target))

    def send_away(self, value):
        def target(d, r, o, i):
            return (d, r, 1 - d, i) if o == d else None

        return lax.ppermute(value, ALL, self.pairs(target))


def dot(left, right):
    return jnp.dot(left, right, preferred_element_type=F32)


def dot_t(left, right):
    return lax.dot_general(left, right, (((1,), (1,)), ((), ())), preferred_element_type=F32)


def t_dot(left, right):
    return lax.dot_general(left, right, (((0,), (0,)), ((), ())), preferred_element_type=F32)


def norm_forward(hidden, gain, shift):
    row_mean = jnp.mean(hidden, axis=1, keepdims=True)
    variance = jnp.mean(hidden * hidden, axis=1, keepdims=True) - row_mean * row_mean
    inverse = lax.rsqrt(variance + NORM_EPSILON)
    normed = (hidden - row_mean) * inverse
    return (normed * gain + shift, normed, inverse)


def norm_backward(grad_after, normed, inverse, gain):
    grad_normed = grad_after * gain
    mean_one = jnp.mean(grad_normed, axis=1, keepdims=True)
    mean_two = jnp.mean(grad_normed * normed, axis=1, keepdims=True)
    return inverse * (grad_normed - mean_one - normed * mean_two)


def head_groups(width):
    columns = min(128, width)
    return columns, columns // HD, width // columns


def attend_forward_kernel(width, block, qkv, ids_row, ids_col, out):
    length = qkv.shape[1]
    columns, per_group, groups = head_groups(width)
    lane = lax.broadcasted_iota(jnp.int32, (block, columns), 1) // HD

    @pl.loop(0, length // block)
    def _(step):
        rows = pl.ds(pl.multiple_of(step * block, block), block)
        same = ids_col[0, rows, :] == ids_row[0]
        for group in range(groups):
            first = group * columns
            queries = qkv[0, rows, first : first + columns]
            keys = qkv[0, :, width + first : width + first + columns]
            values = qkv[0, :, 2 * width + first : 2 * width + first + columns]
            result = None
            for head in range(per_group):
                masked = jnp.where(lane == head, queries, jnp.zeros_like(queries))
                scores = jnp.where(same, dot_t(masked, keys), HIDDEN_SCORE)
                top = jnp.max(scores, axis=1, keepdims=True)
                terms = jnp.exp2((scores - top) * EXP2_SCALE)
                total = jnp.sum(terms, axis=1, keepdims=True)
                part = dot(terms.astype(BF), values) / total
                result = part if result is None else jnp.where(lane == head, part, result)
            out[0, rows, first : first + columns] = result.astype(BF)


def attend_backward_kernel(width, block, qkv, grads, ids_row, ids_col, out, key_total, value_total):
    length = qkv.shape[1]
    columns, per_group, groups = head_groups(width)
    lane = lax.broadcasted_iota(jnp.int32, (block, columns), 1) // HD
    key_lane = lax.broadcasted_iota(jnp.int32, (length, columns), 1) // HD
    for group in range(groups):
        first = group * columns
        keys = qkv[0, :, width + first : width + first + columns]
        values = qkv[0, :, 2 * width + first : 2 * width + first + columns]
        key_total[...] = jnp.zeros_like(key_total)
        value_total[...] = jnp.zeros_like(value_total)

        @pl.loop(0, length // block)
        def _(step):
            rows = pl.ds(pl.multiple_of(step * block, block), block)
            same = ids_col[0] == ids_row[0, :, rows]
            queries = qkv[0, rows, first : first + columns]
            tops = grads[0, rows, first : first + columns]
            query_grad = None
            for head in range(per_group):
                own = lane == head
                head_queries = jnp.where(own, queries, jnp.zeros_like(queries))
                head_grads = jnp.where(own, tops, jnp.zeros_like(tops))
                head_keys = jnp.where(key_lane == head, keys, jnp.zeros_like(keys))
                scores = jnp.where(same, dot_t(keys, head_queries), HIDDEN_SCORE)
                top = jnp.max(scores, axis=0, keepdims=True)
                terms = jnp.exp2((scores - top) * EXP2_SCALE)
                probs = terms * (1.0 / jnp.sum(terms, axis=0, keepdims=True))
                prob_grads = dot_t(values, head_grads)
                inner = jnp.sum(probs * prob_grads, axis=0, keepdims=True)
                score_grads = (probs * (prob_grads - inner)).astype(BF)
                value_total[...] += dot(probs.astype(BF), head_grads)
                key_total[...] += dot(score_grads, head_queries)
                part = t_dot(score_grads, head_keys)
                query_grad = part if query_grad is None else query_grad + part
            out[0, rows, first : first + columns] = (query_grad * SCALE).astype(BF)

        out[0, :, width + first : width + first + columns] = (key_total[...] * SCALE).astype(BF)
        out[0, :, 2 * width + first : 2 * width + first + columns] = value_total[...].astype(BF)


def whole_block(shape):
    return pl.BlockSpec((1,) + shape[1:], lambda s: (s, 0, 0))


def attend_forward(qkv, ids):
    count, length, columns = qkv.shape
    width = columns // 3
    ids_row, ids_col = ids[:, None, :], ids[:, :, None]
    return pl.pallas_call(
        partial(attend_forward_kernel, width, min(256, length)),
        grid=(count,),
        in_specs=[whole_block(v.shape) for v in (qkv, ids_row, ids_col)],
        out_specs=whole_block((count, length, width)),
        out_shape=jax.ShapeDtypeStruct((count, length, width), BF),
        compiler_params=pltpu.CompilerParams(vmem_limit_bytes=48 * 1024 * 1024),
        cost_estimate=pl.CostEstimate(
            flops=4 * count * length * length * 2 * width,
            bytes_accessed=count * length * width * 8,
            transcendentals=count * length * length * (width // HD),
        ),
    )(qkv, ids_row, ids_col)


def attend_backward(qkv, grads, ids):
    count, length, columns = qkv.shape
    width = columns // 3
    group = head_groups(width)[0]
    ids_row, ids_col = ids[:, None, :], ids[:, :, None]
    return pl.pallas_call(
        partial(attend_backward_kernel, width, min(256, length)),
        grid=(count,),
        in_specs=[whole_block(v.shape) for v in (qkv, grads, ids_row, ids_col)],
        out_specs=whole_block((count, length, columns)),
        out_shape=jax.ShapeDtypeStruct((count, length, columns), BF),
        scratch_shapes=[pltpu.VMEM((length, group), F32)] * 2,
        compiler_params=pltpu.CompilerParams(vmem_limit_bytes=48 * 1024 * 1024),
        cost_estimate=pl.CostEstimate(
            flops=10 * count * length * length * 2 * width,
            bytes_accessed=count * length * width * 14,
            transcendentals=count * length * length * (width // HD),
        ),
    )(qkv, grads, ids_row, ids_col)


D_AX, R_AX, O_AX, I_AX = 0, 1, 2, 3


def gelu_pair(value):
    cdf = 0.5 * (1.0 + lax.erf(value * (0.5**0.5)))
    density = jnp.exp(-0.5 * value * value) * (1.0 / math.sqrt(2.0 * math.pi))
    return value * cdf, cdf + value * density


def on_device(
    sizes,
    tokens,
    segment_ids,
    in_weight,
    in_bias,
    out_weight,
    out_bias,
    gain_one,
    shift_one,
    up_weight,
    up_bias,
    down_weight,
    down_bias,
    gain_two,
    shift_two,
    cotangent,
):
    n_dp, n_row, n_col = sizes
    rows_here, model = tokens.shape
    n_outer, length = segment_ids.shape
    n_inner = length // rows_here
    assert n_dp == 2 and n_outer == 2 and n_outer * n_inner == n_col
    net = Grid(n_dp, n_row, n_outer, n_inner)
    d, r, c = (lax.axis_index(name) for name in ALL)
    o, i = c // n_inner, c % n_inner
    at_home = o == d
    width = in_weight.shape[1] // 3
    heads = width // HD
    part = model // n_row
    units = up_weight.shape[1]
    half = units // 2

    def place(value):
        return lax.rem(r - value + n_row, n_row)

    def gather_row(value, axis):
        shape = list(value.shape)
        step = shape[axis]
        shape[axis] = step * n_row
        result = jnp.zeros(shape, value.dtype)
        for k in range(n_row):
            block = value if k == 0 else net.shift(value, R_AX, k)
            result = lax.dynamic_update_slice_in_dim(result, block, place(k) * step, axis)
        return result

    def scatter_row(value, axis):
        step = value.shape[axis] // n_row
        own = lax.dynamic_slice_in_dim(value, r * step, step, axis).astype(F32)
        for k in range(1, n_row):
            block = lax.dynamic_slice_in_dim(value, place(k) * step, step, axis)
            own = own + net.shift(block.astype(BF), R_AX, -k).astype(F32)
        return own

    def gather_units(value):
        blocks = [value] + [net.shift(value, I_AX, k) for k in range(1, n_inner)]
        blocks = jnp.stack(blocks)
        return jnp.stack([blocks] + [net.shift(blocks, O_AX, k) for k in range(1, n_outer)])

    def scatter_units(value, kind):
        own = value[0].astype(F32)
        for k in range(1, n_outer):
            own = own + net.shift(value[k].astype(kind), O_AX, -k).astype(F32)
        result = own[0]
        for k in range(1, n_inner):
            result = result + net.shift(own[k].astype(kind), I_AX, -k).astype(F32)
        return result

    def other(value):
        return net.shift(value, D_AX, 1)

    def at_block(value):
        return jnp.where(at_home, value, net.send_away(value))

    def from_block(value, kind):
        summed = value + net.send_home(value.astype(kind)).astype(F32)
        return jnp.where(at_home, summed, other(summed))

    in_mine = in_weight.reshape(part, heads, 3, HD).transpose(0, 2, 1, 3).reshape(part, 3 * width)
    in_full = gather_row(at_block(in_mine), 0)
    out_full = gather_row(at_block(out_weight), 1)
    bias_rows = at_block(in_bias).reshape(heads, 2, HD)
    in_bias_row = jnp.concatenate(
        [bias_rows[:, 0].reshape(width), jnp.zeros((width,), F32), bias_rows[:, 1].reshape(width)]
    )
    up_blocks = gather_units(
        gather_row(lax.dynamic_slice_in_dim(up_weight, d * half, half, 1), 0)
    ).reshape(n_col, model, half)
    down_blocks = gather_units(
        gather_row(lax.dynamic_slice_in_dim(down_weight, d * half, half, 0), 1)
    ).reshape(n_col, half, model)
    up_full = jnp.concatenate([up_blocks[k] for k in range(n_col)], axis=1)
    down_full = down_blocks.reshape(n_col * half, model)
    up_bias_row = gather_units(lax.dynamic_slice_in_dim(up_bias, d * half, half, 0)).reshape(
        n_col * half
    )

    def spread(value):
        parts = [value] + [net.shift(value, I_AX, k) for k in range(1, n_inner)]
        return jnp.concatenate(parts + [other(v) for v in parts], axis=0)

    def collect(value, weights_of):
        pieces = value.reshape(2, n_inner, rows_here, value.shape[-1])
        arrived = [
            other(weights_of(pieces[1, k]).astype(BF)) for k in reversed(range(n_inner))
        ][::-1]
        result = None
        for k in range(1, n_inner):
            one = weights_of(pieces[0, k]) + arrived[k].astype(F32)
            moved = net.shift(one.astype(BF), I_AX, -k).astype(F32)
            result = moved if result is None else result + moved
        own = weights_of(pieces[0, 0]) + arrived[0].astype(F32)
        return own if result is None else own + result

    own_ids = lax.dynamic_index_in_dim(segment_ids, o, 0, keepdims=False)
    own_ids = jnp.concatenate(
        [
            lax.dynamic_slice_in_dim(
                own_ids, lax.rem(i - k + n_inner, n_inner) * rows_here, rows_here, 0
            )
            for k in range(n_inner)
        ]
    )
    ids = jnp.stack([own_ids, other(own_ids)])

    token_full = spread(tokens)
    projected = (dot(token_full, in_full) + in_bias_row).astype(BF)
    projected = projected.reshape(2, length, 3 * width)
    attended = attend_forward(projected, ids).reshape(2 * length, width)
    branch = collect(attended, lambda v: dot(v, out_full))
    residual_one = tokens.astype(F32) + (branch + out_bias)
    normed_one, unit_one, inverse_one = norm_forward(residual_one, gain_one, shift_one)

    def both(value):
        return jnp.concatenate([value, other(value)], axis=0)

    def across(value, weights_of):
        away = other(weights_of(value[rows_here:]).astype(BF))
        return weights_of(value[:rows_here]) + away.astype(F32)

    mid = both(normed_one.astype(BF))
    hidden, slope = gelu_pair(dot(mid, up_full) + up_bias_row)
    hidden, slope = hidden.astype(BF), slope.astype(BF)
    residual_two = normed_one + (across(hidden, lambda v: dot(v, down_full)) + down_bias)
    normed_two, unit_two, inverse_two = norm_forward(residual_two, gain_two, shift_two)
    output = normed_two.astype(BF)

    grad_top = cotangent.astype(F32)
    grad_gain_two = jnp.sum(grad_top * unit_two, axis=0)
    grad_shift_two = jnp.sum(grad_top, axis=0)
    grad_two = norm_backward(grad_top, unit_two, inverse_two, gain_two)
    grad_two_low = grad_two.astype(BF)
    grad_down_bias = jnp.sum(grad_two_low.astype(F32), axis=0)
    grad_two_both = both(grad_two_low)
    grad_pre = (dot_t(grad_two_both, down_full) * slope.astype(F32)).astype(BF)
    grad_one = grad_two + across(grad_pre, lambda v: dot_t(v, up_full))
    grad_down = t_dot(hidden, grad_two_both).reshape(n_outer, n_inner, half, model)
    grad_up = jnp.stack(
        [t_dot(mid, grad_pre[:, k * half : (k + 1) * half]) for k in range(n_col)]
    ).reshape(n_outer, n_inner, model, half)
    grad_up_bias = jnp.sum(grad_pre.astype(F32), axis=0).reshape(n_outer, n_inner, half)

    grad_gain_one = jnp.sum(grad_one * unit_one, axis=0)
    grad_shift_one = jnp.sum(grad_one, axis=0)
    grad_first = norm_backward(grad_one, unit_one, inverse_one, gain_one)
    grad_first_low = grad_first.astype(BF)
    grad_out_bias = jnp.sum(grad_first_low.astype(F32), axis=0)
    full_sums = net.total(
        jnp.stack(
            [
                grad_out_bias,
                grad_gain_one,
                grad_shift_one,
                grad_down_bias,
                grad_gain_two,
                grad_shift_two,
            ]
        )
    )

    grad_first_full = spread(grad_first_low)
    grad_attended = dot_t(grad_first_full, out_full).astype(BF).reshape(2, length, width)
    grad_projected = attend_backward(projected, grad_attended, ids).reshape(
        2 * length, 3 * width
    )
    grad_tokens = grad_first + collect(grad_projected, lambda v: dot_t(v, in_full))
    grad_out = t_dot(attended, grad_first_full)
    grad_in = t_dot(token_full, grad_projected)
    bias_terms = jnp.sum(grad_projected.astype(F32), axis=0).reshape(3, heads, HD)
    grad_in_bias = jnp.stack([bias_terms[0], bias_terms[2]], axis=1).reshape(2 * width)

    def row_total(value):
        bit = 1
        while bit < n_row:
            value = value + net.flip(value, R_AX, bit)
            bit *= 2
        return value

    def join_halves(value, axis):
        there = other(value)
        first = jnp.where(d == 0, value, there)
        second = jnp.where(d == 0, there, value)
        return jnp.concatenate([first, second], axis=axis)

    grad_down = join_halves(scatter_row(scatter_units(grad_down, BF), 1), 0)
    grad_up = join_halves(scatter_row(scatter_units(grad_up, BF), 0), 1)
    grad_up_bias = join_halves(row_total(scatter_units(grad_up_bias, F32)), 0)
    grad_out = from_block(scatter_row(grad_out, 1), BF)
    grad_in = from_block(scatter_row(grad_in, 0), BF)
    grad_in = grad_in.reshape(part, 3, heads, HD).transpose(0, 2, 1, 3).reshape(part, 3 * width)
    grad_in_bias = from_block(row_total(grad_in_bias), F32)
    return (
        output,
        grad_tokens,
        grad_in,
        grad_in_bias,
        grad_out,
        full_sums[0],
        full_sums[1],
        full_sums[2],
        grad_up,
        grad_up_bias,
        grad_down,
        full_sums[3],
        full_sums[4],
        full_sums[5],
    )


def solution(mesh):
    return jax.shard_map(
        partial(on_device, tuple(mesh.shape[name] for name in ALL)),
        mesh=mesh,
        in_specs=(
            P(("dp", "row", "col"), None),
            P(("dp", "row"), None),
            P("row", "col"),
            P("col"),
            P("col", "row"),
            P(),
            P(),
            P(),
            P("row", "col"),
            P("col"),
            P("col", "row"),
            P(),
            P(),
            P(),
            P(("dp", "row", "col"), None),
        ),
        out_specs=(
            P(("dp", "row", "col"), None),
            P(("dp", "row", "col"), None),
            P("row", "col"),
            P("col"),
            P("col", "row"),
            P(),
            P(),
            P(),
            P("row", "col"),
            P("col"),
            P("col", "row"),
            P(),
            P(),
            P(),
        ),
        check_vma=False,
    )
```

```python
from functools import partial
import math

import jax
import jax.numpy as jnp
from jax import lax
from jax.experimental import pallas as pl
from jax.experimental.pallas import tpu as pltpu
from jax.sharding import PartitionSpec as P

HD = 64
NORM_EPSILON = 1e-12
ALL = ("dp", "row", "col")
BF = jnp.bfloat16
F32 = jnp.float32
HIDDEN_SCORE = -1e30
SCALE = HD ** (-0.5)
EXP2_SCALE = SCALE * math.log2(math.e)


class Grid:
    def __init__(self, dp, row, outer, inner):
        self.shape = (dp, row, outer, inner)

    def pairs(self, target):
        n_d, n_r, n_o, n_i = self.shape

        def flat(d, r, o, i):
            return ((d * n_r + r) * n_o + o) * n_i + i

        result = []
        for d in range(n_d):
            for r in range(n_r):
                for o in range(n_o):
                    for i in range(n_i):
                        there = target(d, r, o, i)
                        if there is not None:
                            result.append((flat(d, r, o, i), flat(*there)))
        return result

    def shift(self, value, axis, by):
        size = self.shape[axis]

        def target(*at):
            at = list(at)
            at[axis] = (at[axis] + by) % size
            return tuple(at)

        return lax.ppermute(value, ALL, self.pairs(target))

    def flip(self, value, axis, bit):
        def target(*at):
            at = list(at)
            at[axis] = at[axis] ^ bit
            return tuple(at)

        return lax.ppermute(value, ALL, self.pairs(target))

    def total(self, value):
        for axis in (0, 3, 2, 1):
            size = self.shape[axis]
            bit = 1
            while bit < size:
                value = value + self.flip(value, axis, bit)
                bit *= 2
        return value


def dot(left, right):
    return jnp.dot(left, right, preferred_element_type=F32)


def dot_t(left, right):
    return lax.dot_general(left, right, (((1,), (1,)), ((), ())), preferred_element_type=F32)


def t_dot(left, right):
    return lax.dot_general(left, right, (((0,), (0,)), ((), ())), preferred_element_type=F32)


def after(value, *earlier):
    return lax.optimization_barrier((value, *earlier))[0]


def norm_forward(hidden, gain, shift):
    row_mean = jnp.mean(hidden, axis=1, keepdims=True)
    variance = jnp.mean(hidden * hidden, axis=1, keepdims=True) - row_mean * row_mean
    inverse = lax.rsqrt(variance + NORM_EPSILON)
    normed = (hidden - row_mean) * inverse
    return (normed * gain + shift, normed, inverse)


def norm_backward(grad_after, normed, inverse, gain):
    grad_normed = grad_after * gain
    mean_one = jnp.mean(grad_normed, axis=1, keepdims=True)
    mean_two = jnp.mean(grad_normed * normed, axis=1, keepdims=True)
    return inverse * (grad_normed - mean_one - normed * mean_two)


def head_groups(width):
    columns = min(128, width)
    return columns, columns // HD, width // columns


def attend_forward_kernel(width, block, qkv, ids_row, ids_col, *rest):
    out = rest[-1]
    length = qkv.shape[1]
    columns, per_group, groups = head_groups(width)
    lane = lax.broadcasted_iota(jnp.int32, (block, columns), 1) // HD

    @pl.loop(0, length // block)
    def _(step):
        rows = pl.ds(pl.multiple_of(step * block, block), block)
        same = ids_col[0, rows, :] == ids_row[0]
        for group in range(groups):
            first = group * columns
            queries = qkv[0, rows, first : first + columns]
            keys = qkv[0, :, width + first : width + first + columns]
            values = qkv[0, :, 2 * width + first : 2 * width + first + columns]
            result = None
            for head in range(per_group):
                masked = jnp.where(lane == head, queries, jnp.zeros_like(queries))
                scores = jnp.where(same, dot_t(masked, keys), HIDDEN_SCORE)
                top = jnp.max(scores, axis=1, keepdims=True)
                terms = jnp.exp2((scores - top) * EXP2_SCALE)
                total = jnp.sum(terms, axis=1, keepdims=True)
                part = dot(terms.astype(BF), values) / total
                result = part if result is None else jnp.where(lane == head, part, result)
            out[0, rows, first : first + columns] = result.astype(BF)


def attend_backward_kernel(width, block, qkv, grads, ids_row, ids_col, *rest):
    out, key_total, value_total = rest[-3:]
    length = qkv.shape[1]
    columns, per_group, groups = head_groups(width)
    lane = lax.broadcasted_iota(jnp.int32, (block, columns), 1) // HD
    key_lane = lax.broadcasted_iota(jnp.int32, (length, columns), 1) // HD
    for group in range(groups):
        first = group * columns
        keys = qkv[0, :, width + first : width + first + columns]
        values = qkv[0, :, 2 * width + first : 2 * width + first + columns]
        key_total[...] = jnp.zeros_like(key_total)
        value_total[...] = jnp.zeros_like(value_total)

        @pl.loop(0, length // block)
        def _(step):
            rows = pl.ds(pl.multiple_of(step * block, block), block)
            same = ids_col[0] == ids_row[0, :, rows]
            queries = qkv[0, rows, first : first + columns]
            tops = grads[rows, first : first + columns]
            query_grad = None
            for head in range(per_group):
                own = lane == head
                head_queries = jnp.where(own, queries, jnp.zeros_like(queries))
                head_grads = jnp.where(own, tops, jnp.zeros_like(tops))
                head_keys = jnp.where(key_lane == head, keys, jnp.zeros_like(keys))
                scores = jnp.where(same, dot_t(keys, head_queries), HIDDEN_SCORE)
                top = jnp.max(scores, axis=0, keepdims=True)
                terms = jnp.exp2((scores - top) * EXP2_SCALE)
                probs = terms * (1.0 / jnp.sum(terms, axis=0, keepdims=True))
                prob_grads = dot_t(values, head_grads)
                inner = jnp.sum(probs * prob_grads, axis=0, keepdims=True)
                score_grads = (probs * (prob_grads - inner)).astype(BF)
                value_total[...] += dot(probs.astype(BF), head_grads)
                key_total[...] += dot(score_grads, head_queries)
                part = t_dot(score_grads, head_keys)
                query_grad = part if query_grad is None else query_grad + part
            out[rows, first : first + columns] = (query_grad * SCALE).astype(BF)

        out[:, width + first : width + first + columns] = (key_total[...] * SCALE).astype(BF)
        out[:, 2 * width + first : 2 * width + first + columns] = value_total[...].astype(BF)


def whole_block(shape):
    return pl.BlockSpec((1,) + shape[1:], lambda s: (s, 0, 0))


def attend_forward(qkv, ids, earlier):
    count, length, columns = qkv.shape
    width = columns // 3
    ids_row, ids_col = ids[:, None, :], ids[:, :, None]
    return pl.pallas_call(
        partial(attend_forward_kernel, width, min(256, length)),
        grid=(count,),
        in_specs=[whole_block(v.shape) for v in (qkv, ids_row, ids_col)]
        + [pl.BlockSpec(memory_space=pl.ANY)] * len(earlier),
        out_specs=whole_block((count, length, width)),
        out_shape=jax.ShapeDtypeStruct((count, length, width), BF),
        compiler_params=pltpu.CompilerParams(vmem_limit_bytes=48 * 1024 * 1024),
        cost_estimate=pl.CostEstimate(flops=1024, bytes_accessed=1024, transcendentals=0),
    )(qkv, ids_row, ids_col, *earlier)


def attend_backward(qkv, grads, ids, which, earlier):
    _, length, columns = qkv.shape
    width = columns // 3
    group = head_groups(width)[0]
    ids_row, ids_col = ids[:, None, :], ids[:, :, None]

    def chosen(value):
        return pl.BlockSpec((1,) + value.shape[1:], lambda s: (which, 0, 0))

    return pl.pallas_call(
        partial(attend_backward_kernel, width, min(256, length)),
        grid=(1,),
        in_specs=[chosen(qkv), pl.BlockSpec((length, width), lambda s: (0, 0))]
        + [chosen(ids_row), chosen(ids_col)]
        + [pl.BlockSpec(memory_space=pl.ANY)] * len(earlier),
        out_specs=pl.BlockSpec((length, columns), lambda s: (0, 0)),
        out_shape=jax.ShapeDtypeStruct((length, columns), BF),
        scratch_shapes=[pltpu.VMEM((length, group), F32)] * 2,
        compiler_params=pltpu.CompilerParams(vmem_limit_bytes=48 * 1024 * 1024),
        cost_estimate=pl.CostEstimate(flops=1024, bytes_accessed=1024, transcendentals=0),
    )(qkv, grads, ids_row, ids_col, *earlier)


D_AX, R_AX, O_AX, I_AX = 0, 1, 2, 3


def gelu_pair(value):
    cdf = 0.5 * (1.0 + lax.erf(value * (0.5**0.5)))
    density = jnp.exp(-0.5 * value * value) * (1.0 / math.sqrt(2.0 * math.pi))
    return value * cdf, cdf + value * density


def on_device(
    sizes,
    tokens,
    segment_ids,
    in_weight,
    in_bias,
    out_weight,
    out_bias,
    gain_one,
    shift_one,
    up_weight,
    up_bias,
    down_weight,
    down_bias,
    gain_two,
    shift_two,
    cotangent,
):
    n_dp, n_row, n_col = sizes
    rows_here, model = tokens.shape
    n_outer, length = segment_ids.shape
    n_inner = length // rows_here
    assert n_dp == 2 and n_outer == 2 and n_outer * n_inner == n_col
    net = Grid(n_dp, n_row, n_outer, n_inner)
    d, r, c = (lax.axis_index(name) for name in ALL)
    o, i = c // n_inner, c % n_inner
    at_home = o == d
    width = in_weight.shape[1] // 3
    heads = width // HD
    part = model // n_row
    units = up_weight.shape[1]
    half = units // 2

    def place(k):
        return lax.rem(r - k + n_row, n_row)

    def other(value):
        return net.shift(value, D_AX, 1)

    def across_outer(value):
        return net.shift(value, O_AX, 1)

    def in_order(mine, theirs, axis):
        first = jnp.where(d == 0, mine, theirs)
        second = jnp.where(d == 0, theirs, mine)
        return jnp.concatenate([first, second], axis=axis)

    def gather_row(value, axis):
        shape = list(value.shape)
        step = shape[axis]
        shape[axis] = step * n_row
        result = jnp.zeros(shape, value.dtype)
        for k in range(n_row):
            block = value if k == 0 else net.shift(value, R_AX, k)
            result = lax.dynamic_update_slice_in_dim(result, block, place(k) * step, axis)
        return result

    def scatter_row(value, axis):
        step = value.shape[axis] // n_row
        own = lax.dynamic_slice_in_dim(value, r * step, step, axis).astype(F32)
        for k in range(1, n_row):
            block = lax.dynamic_slice_in_dim(value, place(k) * step, step, axis)
            own = own + net.shift(block.astype(BF), R_AX, -k).astype(F32)
        return own

    def gather_near(value):
        near = [value] + [net.shift(value, I_AX, k) for k in range(1, n_inner)]
        return near + [across_outer(value)]

    def gather_far(near, outer_share):
        near, away = near[:n_inner], near[n_inner]
        cut = int(away.shape[0] * outer_share)
        far = []
        for k in range(1, n_inner):
            pieces = [across_outer(near[k][:cut])]
            if cut < away.shape[0]:
                pieces.append(net.shift(away[cut:], I_AX, k))
            far.append(jnp.concatenate(pieces, axis=0))
        return near + [away] + far

    def scatter_far(blocks):
        near, far = blocks[:n_inner], blocks[n_inner:]
        cut = near[0].shape[0] // 2
        result, away = [near[0]], far[0]
        top, bottom = away[:cut], away[cut:]
        for k in range(1, n_inner):
            low = far[k].astype(BF)
            passed = across_outer(low[:cut]).astype(F32)
            bottom = bottom + net.shift(low[cut:], I_AX, -k).astype(F32)
            result.append(
                jnp.concatenate([near[k][:cut] + passed, near[k][cut:]], axis=0).astype(BF)
            )
        return result + [jnp.concatenate([top, bottom], axis=0).astype(BF)]

    def scatter_near(blocks):
        own = blocks[0] + across_outer(blocks[n_inner]).astype(F32)
        for k in range(1, n_inner):
            own = own + net.shift(blocks[k], I_AX, -k).astype(F32)
        return own

    def exchange_blocks(value, away):
        keep = jnp.where(at_home, value, away)
        return keep, other(jnp.where(at_home, away, value))

    def return_blocks(mine, theirs):
        received = other(theirs).astype(F32)
        keep = jnp.where(at_home, mine, received)
        away = jnp.where(at_home, received, mine)
        return keep + across_outer(away.astype(BF)).astype(F32)

    def join(value, axis):
        return in_order(value, other(value), axis)

    small = jnp.concatenate([in_bias, up_bias])
    small_near = gather_near(small)
    small_blocks = gather_far(small_near, 1.0)
    in_mine = in_weight.reshape(2, part // 2, heads, 3, HD)
    in_mine = lax.dynamic_index_in_dim(in_mine, d, 0, keepdims=False)
    in_mine = in_mine.transpose(0, 2, 1, 3).reshape(part // 2, 3 * width)
    in_row = gather_row(in_mine, 0)
    token_parts = [tokens]
    for k in range(1, n_inner):
        token_parts.append(net.shift(after(tokens, *small_near), I_AX, k))
    in_row, small_blocks = lax.optimization_barrier((in_row, small_blocks))
    in_away = across_outer(in_row)
    in_row, in_away, token_parts = lax.optimization_barrier((in_row, in_away, token_parts))
    in_halves = exchange_blocks(in_row, in_away)
    out_weight = after(out_weight, in_row)
    bias_rows = jnp.where(
        at_home, small_blocks[0][: 2 * width], small_blocks[n_inner][: 2 * width]
    ).reshape(heads, 2, HD)
    in_bias_row = jnp.concatenate(
        [bias_rows[:, 0].reshape(width), jnp.zeros((width,), F32), bias_rows[:, 1].reshape(width)]
    )
    up_bias_blocks = [
        lax.dynamic_slice_in_dim(v[2 * width :], d * half, half, 0) for v in small_blocks
    ]
    in_full = in_order(
        *(v.reshape(n_row, 1, part // 2, 3 * width) for v in in_halves), 1
    ).reshape(model, 3 * width)
    out_mine = lax.dynamic_slice_in_dim(out_weight, d * (width // 2), width // 2, 0)
    out_row = gather_row(out_mine, 1)
    out_away = across_outer(after(out_row, in_away))
    out_full = in_order(*exchange_blocks(out_row, out_away), 0)
    up_mine = lax.dynamic_slice_in_dim(up_weight, d * half, half, 1)
    up_row = gather_row(after(up_mine, out_row), 0)
    up_near = gather_near(after(up_row, out_away))
    def spread(parts):
        return jnp.concatenate(parts, axis=0), jnp.concatenate([other(v) for v in parts], axis=0)

    def collect(own_rows, other_rows, weights_of):
        own_rows, other_rows = (
            v.reshape(n_inner, rows_here, v.shape[-1]) for v in (own_rows, other_rows)
        )
        arrived = [other(weights_of(v).astype(BF)) for v in other_rows]
        result = None
        for k in range(1, n_inner):
            one = weights_of(own_rows[k]) + arrived[k].astype(F32)
            moved = net.shift(one.astype(BF), I_AX, -k).astype(F32)
            result = moved if result is None else result + moved
        own = weights_of(own_rows[0]) + arrived[0].astype(F32)
        return own if result is None else own + result

    own_ids = lax.dynamic_index_in_dim(segment_ids, o, 0, keepdims=False)
    own_ids = jnp.concatenate(
        [
            lax.dynamic_slice_in_dim(
                own_ids, lax.rem(i - k + n_inner, n_inner) * rows_here, rows_here, 0
            )
            for k in range(n_inner)
        ]
    )
    ids = jnp.stack([own_ids, other(own_ids)])

    token_full = jnp.concatenate(spread(token_parts), axis=0)
    projected = (dot(token_full, in_full) + in_bias_row).astype(BF)
    projected = projected.reshape(2, length, 3 * width)
    down_mine = lax.dynamic_slice_in_dim(down_weight, d * half, half, 0)
    down_row = gather_row(after(down_mine, projected), 1)
    attended = attend_forward(projected, ids, (up_row,))
    attended, up_near, down_row = lax.optimization_barrier((attended, up_near, down_row))
    down_away = across_outer(down_row)
    branch = collect(attended[0], attended[1], lambda v: dot(v, out_full))
    token_late = after(token_full, attended)
    step = part // 2
    halves_of = [
        jnp.concatenate(
            [token_late[:, k * step : (k + 1) * step] for k in range(at, 2 * n_row, 2)], axis=1
        )
        for at in range(2)
    ]
    token_halves = (
        jnp.where(d == 0, halves_of[0], halves_of[1]),
        jnp.where(d == 0, halves_of[1], halves_of[0]),
    )
    branch, down_away, token_halves = lax.optimization_barrier((branch, down_away, token_halves))
    up_blocks = gather_far(up_near, 1.0)
    down_near = gather_near(after(down_row, branch))[:n_inner] + [down_away]
    down_blocks = gather_far(down_near, 0.5)
    residual_one = tokens.astype(F32) + (branch + out_bias)
    normed_one, unit_one, inverse_one = norm_forward(residual_one, gain_one, shift_one)

    def both(value):
        return jnp.concatenate([value, other(value)], axis=0)

    def across(blocks, weights_of):
        def product(start):
            result = None
            for k, value in enumerate(blocks):
                one = weights_of(value[start : start + rows_here], k)
                result = one if result is None else result + one
            return result

        away = other(product(rows_here).astype(BF))
        return product(0) + away.astype(F32)

    mid = both(normed_one.astype(BF))
    hidden, slope = [], []
    for k in range(n_col):
        one = gelu_pair(dot(mid, up_blocks[k]) + up_bias_blocks[k])
        hidden.append(one[0].astype(BF))
        slope.append(one[1].astype(BF))
    residual_two = normed_one + (
        across(hidden, lambda v, k: dot(v, down_blocks[k])) + down_bias
    )
    normed_two, unit_two, inverse_two = norm_forward(residual_two, gain_two, shift_two)
    output = normed_two.astype(BF)

    grad_top = cotangent.astype(F32)
    grad_gain_two = jnp.sum(grad_top * unit_two, axis=0)
    grad_shift_two = jnp.sum(grad_top, axis=0)
    grad_two = norm_backward(grad_top, unit_two, inverse_two, gain_two)
    grad_two_low = grad_two.astype(BF)
    grad_down_bias = jnp.sum(grad_two_low.astype(F32), axis=0)
    grad_two_both = both(grad_two_low)
    grad_down = scatter_far([t_dot(v, grad_two_both) for v in hidden])
    grad_pre = [
        (dot_t(grad_two_both, down_blocks[k]) * slope[k].astype(F32)).astype(BF)
        for k in range(n_col)
    ]
    grad_pre, grad_down = lax.optimization_barrier((grad_pre, grad_down))
    grad_one = grad_two + across(grad_pre, lambda v, k: dot_t(v, up_blocks[k]))
    grad_up_bias = jnp.zeros((2, n_outer, n_inner, half), F32)
    for k in range(n_col):
        there_o = lax.rem(o - k // n_inner + n_outer, n_outer)
        there_i = lax.rem(i - k % n_inner + n_inner, n_inner)
        grad_up_bias = lax.dynamic_update_slice(
            grad_up_bias,
            jnp.sum(grad_pre[k].astype(F32), axis=0)[None, None, None],
            (d, there_o, there_i, 0),
        )

    grad_gain_one = jnp.sum(grad_one * unit_one, axis=0)
    grad_shift_one = jnp.sum(grad_one, axis=0)
    grad_first = norm_backward(grad_one, unit_one, inverse_one, gain_one)
    grad_first_low = grad_first.astype(BF)
    grad_out_bias = jnp.sum(grad_first_low.astype(F32), axis=0)

    first_parts = [grad_first_low]
    first_parts += [net.shift(grad_first_low, I_AX, k) for k in range(1, n_inner)]
    mid_late = after(mid, grad_first_low)
    grad_up = scatter_far([t_dot(mid_late, v) for v in grad_pre])
    grad_first_both = spread(first_parts)
    grad_attended = [dot_t(v, out_full).astype(BF) for v in grad_first_both]

    def halves(value, axis):
        step = value.shape[axis] // 2
        return [
            lax.dynamic_slice_in_dim(value, at * step, step, axis) for at in (d, 1 - d)
        ]

    out_mine, out_theirs = (
        [sum(t_dot(v, w) for v, w in zip(pair, grad_first_both)) for pair in
         zip(*(halves(v, 1) for v in attended))]
    )
    grad_out = return_blocks(out_mine, out_theirs.astype(BF))
    grad_down = scatter_near(grad_down)
    projected_grads = [None, None]
    projected_grads[1] = attend_backward(projected, grad_attended[1], ids, 1, (grad_down,))
    grad_down = scatter_row(grad_down, 1)
    grad_up = scatter_near(lax.optimization_barrier((grad_up, grad_out))[0])
    projected_grads[0] = attend_backward(
        projected, grad_attended[0], ids, 0, (grad_down, grad_out)
    )
    grad_out = scatter_row(grad_out, 1)
    projected_grads[0], grad_up, grad_out = lax.optimization_barrier(
        (projected_grads[0], grad_up, grad_out)
    )
    grad_tokens = grad_first + collect(*projected_grads, lambda v: dot_t(v, in_full))
    in_mine, in_theirs = (
        sum(t_dot(v[k * length : (k + 1) * length], w) for k, w in enumerate(projected_grads))
        for v in token_halves
    )
    grad_in = return_blocks(in_mine, in_theirs.astype(BF))
    grad_up = scatter_row(grad_up, 0)
    grad_in, grad_tokens, grad_up = lax.optimization_barrier((grad_in, grad_tokens, grad_up))
    grad_in_there = grad_in
    grad_in = scatter_row(grad_in, 0)
    bias_terms = sum(jnp.sum(v.astype(F32), axis=0) for v in projected_grads).reshape(3, heads, HD)
    bias_terms = jnp.stack([bias_terms[0], bias_terms[2]], axis=1).reshape(1, 2 * width)
    grad_in_bias = lax.dynamic_update_slice_in_dim(
        jnp.zeros((n_col, 2 * width), F32), bias_terms, d * n_inner + i, 0
    )

    flat = [
        grad_out_bias,
        grad_gain_one,
        grad_shift_one,
        grad_down_bias,
        grad_gain_two,
        grad_shift_two,
        grad_up_bias.reshape(-1),
        grad_in_bias.reshape(-1),
    ]
    flat = after(jnp.concatenate(flat).reshape(-1, 128), grad_in_there)
    sums = net.total(flat).reshape(-1)
    sums = jnp.split(sums, [model * k for k in range(1, 7)] + [6 * model + 2 * n_col * half])
    grad_up_bias = lax.dynamic_index_in_dim(
        sums[6].reshape(2, n_col, half), c, 1, keepdims=False
    ).reshape(2 * half)
    grad_in_bias = lax.dynamic_index_in_dim(
        sums[7].reshape(n_col, 2 * width), c, 0, keepdims=False
    )

    grad_down = join(grad_down, 0)
    grad_up = join(grad_up, 1)
    grad_out = join(grad_out, 0)
    grad_in = join(grad_in, 0)
    grad_in = grad_in.reshape(part, 3, heads, HD).transpose(0, 2, 1, 3).reshape(part, 3 * width)
    return (
        output,
        grad_tokens,
        grad_in,
        grad_in_bias,
        grad_out,
        sums[0],
        sums[1],
        sums[2],
        grad_up,
        grad_up_bias,
        grad_down,
        sums[3],
        sums[4],
        sums[5],
    )


def solution(mesh):
    return jax.shard_map(
        partial(on_device, tuple(mesh.shape[name] for name in ALL)),
        mesh=mesh,
        in_specs=(
            P(("dp", "row", "col"), None),
            P(("dp", "row"), None),
            P("row", "col"),
            P("col"),
            P("col", "row"),
            P(),
            P(),
            P(),
            P("row", "col"),
            P("col"),
            P("col", "row"),
            P(),
            P(),
            P(),
            P(("dp", "row", "col"), None),
        ),
        out_specs=(
            P(("dp", "row", "col"), None),
            P(("dp", "row", "col"), None),
            P("row", "col"),
            P("col"),
            P("col", "row"),
            P(),
            P(),
            P(),
            P("row", "col"),
            P("col"),
            P("col", "row"),
            P(),
            P(),
            P(),
        ),
        check_vma=False,
    )
```

```python
from functools import partial
import math

import jax
import jax.numpy as jnp
from jax import lax
from jax.experimental import pallas as pl
from jax.experimental.pallas import tpu as pltpu
from jax.sharding import PartitionSpec as P

HD = 64
NORM_EPSILON = 1e-12
ALL = ("dp", "row", "col")
BF = jnp.bfloat16
F32 = jnp.float32
HIDDEN_SCORE = -1e30
SCALE = HD ** (-0.5)
EXP2_SCALE = SCALE * math.log2(math.e)


class Grid:
    def __init__(self, dp, row, outer, inner):
        self.shape = (dp, row, outer, inner)

    def pairs(self, target):
        n_d, n_r, n_o, n_i = self.shape

        def flat(d, r, o, i):
            return ((d * n_r + r) * n_o + o) * n_i + i

        result = []
        for d in range(n_d):
            for r in range(n_r):
                for o in range(n_o):
                    for i in range(n_i):
                        there = target(d, r, o, i)
                        if there is not None:
                            result.append((flat(d, r, o, i), flat(*there)))
        return result

    def shift(self, value, axis, by):
        size = self.shape[axis]

        def target(*at):
            at = list(at)
            at[axis] = (at[axis] + by) % size
            return tuple(at)

        return lax.ppermute(value, ALL, self.pairs(target))

    def flip(self, value, axis, bit):
        def target(*at):
            at = list(at)
            at[axis] = at[axis] ^ bit
            return tuple(at)

        return lax.ppermute(value, ALL, self.pairs(target))

    def total(self, value, axes):
        for axis in axes:
            size = self.shape[axis]
            bit = 1
            while bit < size:
                value = value + self.flip(value, axis, bit)
                bit *= 2
        return value


def dot(left, right):
    return jnp.dot(left, right, preferred_element_type=F32)


def dot_t(left, right):
    return lax.dot_general(left, right, (((1,), (1,)), ((), ())), preferred_element_type=F32)


def t_dot(left, right):
    return lax.dot_general(left, right, (((0,), (0,)), ((), ())), preferred_element_type=F32)


def after(value, *earlier):
    return lax.optimization_barrier((value, *earlier))[0]


def norm_forward(hidden, gain, shift):
    row_mean = jnp.mean(hidden, axis=1, keepdims=True)
    variance = jnp.mean(hidden * hidden, axis=1, keepdims=True) - row_mean * row_mean
    inverse = lax.rsqrt(variance + NORM_EPSILON)
    normed = (hidden - row_mean) * inverse
    return (normed * gain + shift, normed, inverse)


def norm_backward(grad_after, normed, inverse, gain):
    grad_normed = grad_after * gain
    mean_one = jnp.mean(grad_normed, axis=1, keepdims=True)
    mean_two = jnp.mean(grad_normed * normed, axis=1, keepdims=True)
    return inverse * (grad_normed - mean_one - normed * mean_two)


def head_groups(width):
    columns = min(128, width)
    return columns, columns // HD, width // columns


def attend_forward_kernel(width, block, qkv, ids_row, ids_col, *rest):
    out, logs = rest[-2:]
    length = qkv.shape[1]
    columns, per_group, groups = head_groups(width)
    lane = lax.broadcasted_iota(jnp.int32, (block, columns), 1) // HD
    log_lane = lax.broadcasted_iota(jnp.int32, (block, 128), 1)

    @pl.loop(0, length // block)
    def _(step):
        rows = pl.ds(pl.multiple_of(step * block, block), block)
        same = ids_col[0, rows, :] == ids_row[0]
        row_logs = jnp.zeros((block, 128), F32)
        for group in range(groups):
            first = 3 * group * columns
            queries = qkv[0, rows, first : first + columns]
            keys = qkv[0, :, first + columns : first + 2 * columns]
            values = qkv[0, :, first + 2 * columns : first + 3 * columns]
            result = None
            for head in range(per_group):
                masked = jnp.where(lane == head, queries, jnp.zeros_like(queries))
                scores = jnp.where(same, dot_t(masked, keys), HIDDEN_SCORE)
                top = jnp.max(scores, axis=1, keepdims=True)
                terms = jnp.exp2((scores - top) * EXP2_SCALE)
                total = jnp.sum(terms, axis=1, keepdims=True)
                part = dot(terms.astype(BF), values) / total
                result = part if result is None else jnp.where(lane == head, part, result)
                log = top * EXP2_SCALE + jnp.log(total) * math.log2(math.e)
                row_logs = jnp.where(log_lane == group * per_group + head, log, row_logs)
            out[0, rows, group * columns : (group + 1) * columns] = result.astype(BF)
        logs[0, :, rows] = row_logs.T[: logs.shape[1]]


def attend_backward_kernel(
    width, block, group, ranges, qkv, grads, attended, logs, ids_row, ids_col, *rest
):
    out, query_total, key_total, value_total = rest[-4:]
    length = qkv.shape[1]
    columns, per_group, groups = head_groups(width)
    blocks = length // block
    sequence = pl.program_id(0)
    lane = lax.broadcasted_iota(jnp.int32, (block, columns), 1) // HD
    pick = lax.broadcasted_iota(jnp.int32, (8, columns), 0)
    pick = (pick == lax.broadcasted_iota(jnp.int32, (8, columns), 1) // HD).astype(F32)
    def low(at):
        return ranges[sequence, 0, at]

    def high(at):
        return ranges[sequence, 1, at]

    first, outer_first = 3 * group * columns, group * columns
    for total in (query_total, key_total, value_total):
        total[...] = jnp.zeros_like(total)

    @pl.loop(0, blocks)
    def _(step):
        rows = pl.ds(pl.multiple_of(step * block, block), block)
        row_ids = ids_row[0, :, rows]
        queries = qkv[0, rows, first : first + columns]
        tops = grads[0, rows, outer_first : outer_first + columns]
        results = attended[0, rows, outer_first : outer_first + columns]
        inner = lax.dot_general(
            pick,
            tops.astype(F32) * results.astype(F32),
            (((1,), (1,)), ((), ())),
            precision=lax.Precision.HIGHEST,
            preferred_element_type=F32,
        )
        nothing = jnp.zeros_like(queries)
        head_queries = [jnp.where(lane == head, queries, nothing) for head in range(per_group)]
        head_grads = [jnp.where(lane == head, tops, nothing) for head in range(per_group)]
        head_logs = [
            logs[0, pl.ds(group * per_group + head, 1), rows] for head in range(per_group)
        ]

        @pl.loop(0, blocks)
        def _(key_step):
            @pl.when((low(step) <= high(key_step)) & (low(key_step) <= high(step)))
            def _():
                at = pl.ds(pl.multiple_of(key_step * block, block), block)
                keys = qkv[0, at, first + columns : first + 2 * columns]
                values = qkv[0, at, first + 2 * columns : first + 3 * columns]
                same = ids_col[0, at, :] == row_ids
                query_part, key_part, value_part = 0.0, 0.0, 0.0
                for head in range(per_group):
                    scores = dot_t(keys, head_queries[head]) * EXP2_SCALE - head_logs[head]
                    probs = jnp.exp2(jnp.where(same, scores, HIDDEN_SCORE))
                    prob_grads = dot_t(values, head_grads[head])
                    score_grads = (probs * (prob_grads - inner[head : head + 1])).astype(BF)
                    head_keys = jnp.where(lane == head, keys, jnp.zeros_like(keys))
                    value_part += dot(probs.astype(BF), head_grads[head])
                    key_part += dot(score_grads, head_queries[head])
                    query_part += t_dot(score_grads, head_keys)
                value_total[at, :] += value_part
                key_total[at, :] += key_part
                query_total[rows, :] += query_part

    out[0, :, :columns] = (query_total[...] * SCALE).astype(BF)
    out[0, :, columns : 2 * columns] = (key_total[...] * SCALE).astype(BF)
    out[0, :, 2 * columns :] = value_total[...].astype(BF)


def whole_block(shape):
    return pl.BlockSpec((1,) + shape[1:], lambda s, *_: (s, 0, 0))


SMALL_COST = pl.CostEstimate(flops=1024, bytes_accessed=1024, transcendentals=0)


def attend_forward(qkv, ids, earlier):
    count, length, columns = qkv.shape
    width = columns // 3
    ids_row, ids_col = ids[:, None, :], ids[:, :, None]
    log_rows = -(-width // HD // 8) * 8
    return pl.pallas_call(
        partial(attend_forward_kernel, width, min(256, length)),
        grid=(count,),
        in_specs=[whole_block(v.shape) for v in (qkv, ids_row, ids_col)]
        + [pl.BlockSpec(memory_space=pl.ANY)] * len(earlier),
        out_specs=[
            whole_block((count, length, width)),
            whole_block((count, log_rows, length)),
        ],
        out_shape=[
            jax.ShapeDtypeStruct((count, length, width), BF),
            jax.ShapeDtypeStruct((count, log_rows, length), F32),
        ],
        compiler_params=pltpu.CompilerParams(vmem_limit_bytes=48 * 1024 * 1024),
        cost_estimate=SMALL_COST,
    )(qkv, ids_row, ids_col, *earlier)


def attend_backward(qkv, grads, attended, logs, ids, group, others):
    count, length, columns = qkv.shape
    width = columns // 3
    wide = head_groups(width)[0]
    block = min(256, length)
    ids_row, ids_col = ids[:, None, :], ids[:, :, None]
    blocked = ids.reshape(count, length // block, block)
    ranges = jnp.stack([jnp.min(blocked, axis=2), jnp.max(blocked, axis=2)], axis=1)
    operands = (qkv, grads, attended, logs, ids_row, ids_col)
    kept = () if others is None else (others,)
    return pl.pallas_call(
        partial(attend_backward_kernel, width, block, group),
        grid_spec=pltpu.PrefetchScalarGridSpec(
            num_scalar_prefetch=1,
            grid=(count,),
            in_specs=[whole_block(v.shape) for v in operands]
            + [pl.BlockSpec(memory_space=pl.ANY)] * len(kept),
            out_specs=pl.BlockSpec((1, length, 3 * wide), lambda s, *_: (s, 0, group)),
            scratch_shapes=[pltpu.VMEM((length, wide), F32)] * 3,
        ),
        out_shape=jax.ShapeDtypeStruct(qkv.shape, BF),
        input_output_aliases={1 + len(operands): 0} if kept else {},
        compiler_params=pltpu.CompilerParams(vmem_limit_bytes=48 * 1024 * 1024),
        cost_estimate=SMALL_COST,
    )(ranges, *operands, *kept)


D_AX, R_AX, O_AX, I_AX = 0, 1, 2, 3


def gelu_pair(value):
    cdf = 0.5 * (1.0 + lax.erf(value * (0.5**0.5)))
    density = jnp.exp(-0.5 * value * value) * (1.0 / math.sqrt(2.0 * math.pi))
    return value * cdf, cdf + value * density


def on_device(
    sizes,
    tokens,
    segment_ids,
    in_weight,
    in_bias,
    out_weight,
    out_bias,
    gain_one,
    shift_one,
    up_weight,
    up_bias,
    down_weight,
    down_bias,
    gain_two,
    shift_two,
    cotangent,
):
    n_dp, n_row, n_col = sizes
    rows_here, model = tokens.shape
    n_outer, length = segment_ids.shape
    n_inner = length // rows_here
    assert n_dp == 2 and n_outer == 2 and n_outer * n_inner == n_col
    net = Grid(n_dp, n_row, n_outer, n_inner)
    d, r, c = (lax.axis_index(name) for name in ALL)
    o, i = c // n_inner, c % n_inner
    at_home = o == d
    width = in_weight.shape[1] // 3
    heads = width // HD
    wide, per_group, groups = head_groups(width)
    part = model // n_row
    units = up_weight.shape[1]
    half = units // 2

    def place(k):
        return lax.rem(r - k + n_row, n_row)

    def other(value):
        return net.shift(value, D_AX, 1)

    def across_outer(value):
        return net.shift(value, O_AX, 1)

    def in_order(mine, theirs, axis):
        first = jnp.where(d == 0, mine, theirs)
        second = jnp.where(d == 0, theirs, mine)
        return jnp.concatenate([first, second], axis=axis)

    def row_blocks(value):
        return [value] + [net.shift(value, R_AX, k) for k in range(1, n_row)]

    def place_rows(blocks, axis):
        shape = list(blocks[0].shape)
        step = shape[axis]
        shape[axis] = step * n_row
        result = jnp.zeros(shape, blocks[0].dtype)
        for k, block in enumerate(blocks):
            result = lax.dynamic_update_slice_in_dim(result, block, place(k) * step, axis)
        return result

    def scatter_row(value, axis):
        step = value.shape[axis] // n_row
        terms = [lax.dynamic_slice_in_dim(value, r * step, step, axis).astype(F32)]
        for k in range(1, n_row):
            block = lax.dynamic_slice_in_dim(value, place(k) * step, step, axis)
            terms.append(net.shift(block.astype(BF), R_AX, -k))
        return terms

    def add_up(terms):
        return sum(v.astype(F32) for v in terms)

    def gather_near(value):
        near = [value] + [net.shift(value, I_AX, k) for k in range(1, n_inner)]
        return near + [across_outer(value)]

    def gather_far(near, outer_share):
        near, away = near[:n_inner], near[n_inner]
        cut = int(away.shape[0] * outer_share)
        far = []
        for k in range(1, n_inner):
            pieces = [across_outer(near[k][:cut])]
            if cut < away.shape[0]:
                pieces.append(net.shift(away[cut:], I_AX, k))
            far.append(jnp.concatenate(pieces, axis=0))
        return near + [away] + far

    def scatter_far(blocks):
        return blocks[: n_inner + 1], [across_outer(v.astype(BF)) for v in blocks[n_inner + 1 :]]

    def scatter_near(parts, first=None, earlier=()):
        blocks, passed = parts
        if first is None:
            first = across_outer(blocks[n_inner].astype(BF))
        terms = [blocks[0], first]
        for k in range(1, n_inner):
            sent = (blocks[k].astype(F32) + passed[k - 1].astype(F32)).astype(BF)
            terms.append(net.shift(after(sent, *earlier), I_AX, -k))
        return terms

    def exchange_blocks(value, away):
        keep = jnp.where(at_home, value, away)
        return keep, other(jnp.where(at_home, away, value))

    def return_blocks(mine, theirs):
        received = other(theirs).astype(F32)
        keep = jnp.where(at_home, mine, received)
        away = jnp.where(at_home, received, mine)
        return keep, away.astype(BF)

    def join(value, axis):
        return in_order(value, other(value), axis)

    small = jnp.concatenate([in_bias, up_bias])
    small_near = gather_near(small)
    small_blocks = gather_far(small_near, 1.0)
    in_mine = in_weight.reshape(2, part // 2, groups, per_group, 3, HD)
    in_mine = lax.dynamic_index_in_dim(in_mine, d, 0, keepdims=False)
    in_mine = in_mine.transpose(0, 1, 3, 2, 4).reshape(part // 2, 3 * width)
    in_row = place_rows(row_blocks(in_mine), 0)
    token_parts = [tokens]
    for k in range(1, n_inner):
        token_parts.append(net.shift(after(tokens, *small_near), I_AX, k))
    in_row, small_blocks = lax.optimization_barrier((in_row, small_blocks))
    out_weight, up_weight = (after(v, in_row) for v in (out_weight, up_weight))
    in_away = across_outer(in_row)
    in_row, in_away, token_parts = lax.optimization_barrier((in_row, in_away, token_parts))
    in_halves = exchange_blocks(in_row, in_away)
    bias_rows = jnp.where(
        at_home, small_blocks[0][: 2 * width], small_blocks[n_inner][: 2 * width]
    ).reshape(groups, per_group, 2, HD)
    in_bias_row = jnp.stack(
        [bias_rows[:, :, 0], jnp.zeros_like(bias_rows[:, :, 0]), bias_rows[:, :, 1]], axis=1
    ).reshape(3 * width)
    up_bias_blocks = [
        lax.dynamic_slice_in_dim(v[2 * width :], d * half, half, 0) for v in small_blocks
    ]
    in_full = in_order(
        *(v.reshape(n_row, 1, part // 2, 3 * width) for v in in_halves), 1
    ).reshape(model, 3 * width)
    out_mine = lax.dynamic_slice_in_dim(out_weight, d * (width // 2), width // 2, 0)
    out_row = place_rows(row_blocks(out_mine), 1)
    out_away = across_outer(after(out_row, in_away))
    up_mine = lax.dynamic_slice_in_dim(up_weight, d * half, half, 1)
    up_row = row_blocks(up_mine)
    def spread(parts):
        return jnp.concatenate(parts, axis=0), jnp.concatenate([other(v) for v in parts], axis=0)

    def collect_here(product):
        arrived = [other(product(1, k).astype(BF)) for k in range(n_inner)]
        sums = [product(0, k) + arrived[k].astype(F32) for k in range(n_inner)]
        return sums[0], [v.astype(BF) for v in sums[1:]]

    def collect(own, sent):
        for k, value in enumerate(sent):
            own = own + net.shift(value, I_AX, -k - 1).astype(F32)
        return own

    def part_rows(k):
        return slice(k * rows_here, (k + 1) * rows_here)

    own_ids = lax.dynamic_index_in_dim(segment_ids, o, 0, keepdims=False)
    own_ids = jnp.concatenate(
        [
            lax.dynamic_slice_in_dim(
                own_ids, lax.rem(i - k + n_inner, n_inner) * rows_here, rows_here, 0
            )
            for k in range(n_inner)
        ]
    )
    ids = jnp.stack([own_ids, other(own_ids)])

    token_full = jnp.concatenate(spread(token_parts), axis=0)
    projected = (dot(token_full, in_full) + in_bias_row).astype(BF)
    projected = projected.reshape(2, length, 3 * width)
    down_mine = lax.dynamic_slice_in_dim(down_weight, d * half, half, 0)
    projected, up_row, out_away = lax.optimization_barrier((projected, up_row, out_away))
    out_full = in_order(*exchange_blocks(out_row, out_away), 0)
    up_row = place_rows(up_row, 0)
    up_near = gather_near(up_row)
    down_row = place_rows(row_blocks(after(down_mine, projected)), 1)
    attended, logs = attend_forward(projected, ids, (up_row,))
    attended, up_near, down_row = lax.optimization_barrier((attended, up_near, down_row))
    down_away = across_outer(down_row)
    branch = collect(*collect_here(lambda seq, k: dot(attended[seq, part_rows(k)], out_full)))
    token_late = after(token_full, attended)
    step = part // 2
    halves_of = [
        jnp.concatenate(
            [token_late[:, k * step : (k + 1) * step] for k in range(at, 2 * n_row, 2)], axis=1
        )
        for at in range(2)
    ]
    token_halves = (
        jnp.where(d == 0, halves_of[0], halves_of[1]),
        jnp.where(d == 0, halves_of[1], halves_of[0]),
    )
    branch, down_away, token_halves = lax.optimization_barrier((branch, down_away, token_halves))
    up_blocks = gather_far(up_near, 1.0)
    down_near = gather_near(after(down_row, branch))[:n_inner] + [down_away]
    down_blocks = gather_far(down_near, 0.5)

    def lay_out(blocks, axis):
        shape = list(blocks[0].shape)
        step = shape[axis]
        shape[axis] = step * len(blocks)
        result = jnp.zeros(shape, blocks[0].dtype)
        for k, block in enumerate(blocks):
            result = lax.dynamic_update_slice_in_dim(result, block, k * step, axis)
        return result

    up_full, down_full = lay_out(up_blocks, 1), lay_out(down_blocks, 0)
    up_bias_row = jnp.concatenate(up_bias_blocks)
    residual_one = tokens.astype(F32) + (branch + out_bias)
    normed_one, unit_one, inverse_one = norm_forward(residual_one, gain_one, shift_one)

    def both(value):
        return jnp.concatenate([value, other(value)], axis=0)

    def across(value, weights_of):
        away = other(weights_of(value[rows_here:]).astype(BF))
        return weights_of(value[:rows_here]) + away.astype(F32)

    mid = both(normed_one.astype(BF))
    hidden, slope = lax.optimization_barrier(
        [v.astype(BF) for v in gelu_pair(dot(mid, up_full) + up_bias_row)]
    )
    residual_two = normed_one + (across(hidden, lambda v: dot(v, down_full)) + down_bias)
    normed_two, unit_two, inverse_two = norm_forward(residual_two, gain_two, shift_two)
    output = normed_two.astype(BF)

    grad_top = cotangent.astype(F32)
    grad_gain_two = jnp.sum(grad_top * unit_two, axis=0)
    grad_shift_two = jnp.sum(grad_top, axis=0)
    grad_two = norm_backward(grad_top, unit_two, inverse_two, gain_two)
    grad_two_low = grad_two.astype(BF)
    grad_down_bias = jnp.sum(grad_two_low.astype(F32), axis=0)
    grad_two_both = both(grad_two_low)

    def unit_blocks(value):
        return [value[k * half : (k + 1) * half] for k in range(n_col)]

    grad_down = scatter_far(unit_blocks(t_dot(hidden, grad_two_both).astype(BF)))
    grad_pre = (dot_t(grad_two_both, down_full) * slope.astype(F32)).astype(BF)
    grad_one = grad_two + across(grad_pre, lambda v: dot_t(v, up_full))
    unit_sums = unit_blocks(jnp.sum(grad_pre.astype(F32), axis=0))
    grad_up_bias = jnp.zeros((2, n_outer, n_inner, half), F32)
    for k in range(n_col):
        there_o = lax.rem(o - k // n_inner + n_outer, n_outer)
        there_i = lax.rem(i - k % n_inner + n_inner, n_inner)
        grad_up_bias = lax.dynamic_update_slice(
            grad_up_bias,
            unit_sums[k][None, None, None],
            (d, there_o, there_i, 0),
        )

    grad_gain_one = jnp.sum(grad_one * unit_one, axis=0)
    grad_shift_one = jnp.sum(grad_one, axis=0)
    grad_first = norm_backward(grad_one, unit_one, inverse_one, gain_one)
    grad_first_low = grad_first.astype(BF)
    grad_out_bias = jnp.sum(grad_first_low.astype(F32), axis=0)

    flat = [
        grad_out_bias,
        grad_gain_one,
        grad_shift_one,
        grad_down_bias,
        grad_gain_two,
        grad_shift_two,
        grad_up_bias.reshape(-1),
    ]
    first_parts = [grad_first_low]
    first_parts += [net.shift(grad_first_low, I_AX, k) for k in range(1, n_inner)]
    down_first = across_outer(grad_down[0][n_inner].astype(BF))
    mid_late = after(mid, grad_first_low, down_first)
    grad_up = scatter_far(unit_blocks(t_dot(grad_pre, mid_late).astype(BF)))
    grad_first_both = spread(first_parts)
    grad_down = scatter_near(grad_down, down_first, first_parts)
    grad_attended = jnp.stack([dot_t(v, out_full).astype(BF) for v in grad_first_both])

    def halves(value, axis):
        step = value.shape[axis] // 2
        return [
            lax.dynamic_slice_in_dim(value, at * step, step, axis) for at in (d, 1 - d)
        ]

    out_mine, out_theirs = (
        [sum(t_dot(v, w) for v, w in zip(pair, grad_first_both)) for pair in
         zip(*(halves(v, 1) for v in attended))]
    )
    grad_out, out_away = return_blocks(out_mine, out_theirs.astype(BF))
    grad_out = [grad_out, across_outer(out_away)]
    projected_grads = None
    for g in range(groups):
        if g == groups - 1:
            grad_attended, grad_down, grad_up, grad_out, projected_grads = (
                lax.optimization_barrier(
                    (grad_attended, grad_down, grad_up, grad_out, projected_grads)
                )
            )
            grad_up = scatter_near(grad_up)
            grad_down = scatter_row(add_up(grad_down), 1)
            grad_out = scatter_row(add_up(grad_out), 1)
        projected_grads = attend_backward(
            projected, grad_attended, attended, logs, ids, g, projected_grads
        )
    projected_grads, grad_up, grad_down, grad_out = lax.optimization_barrier(
        (projected_grads, grad_up, grad_down, grad_out)
    )
    sent = collect_here(lambda seq, k: dot_t(projected_grads[seq, part_rows(k)], in_full))
    in_mine, in_theirs = (
        sum(t_dot(v[k * length : (k + 1) * length], projected_grads[k]) for k in range(2))
        for v in token_halves
    )
    grad_in, in_away = return_blocks(in_mine, in_theirs.astype(BF))
    sent, grad_in, in_away, grad_up, projected_grads = lax.optimization_barrier(
        (sent, grad_in, in_away, grad_up, projected_grads)
    )
    grad_tokens = grad_first + collect(*sent)
    flat = after(jnp.concatenate(flat).reshape(-1, 128), projected_grads)
    sums = net.total(flat, (R_AX, D_AX, O_AX, I_AX)).reshape(-1)
    grad_in = [grad_in, across_outer(in_away)]
    grad_up = scatter_row(add_up(grad_up), 1)
    bias_terms = jnp.sum(projected_grads.astype(F32), axis=(0, 1))
    bias_terms = bias_terms.reshape(groups, 3, per_group, HD)
    bias_terms = jnp.stack([bias_terms[:, 0], bias_terms[:, 2]], axis=2).reshape(1, 2 * width)
    bias_terms = bias_terms + across_outer(bias_terms)
    grad_up, grad_out, grad_tokens, grad_in, bias_terms, sums = lax.optimization_barrier(
        (grad_up, grad_out, grad_tokens, grad_in, bias_terms, sums)
    )
    grad_in = add_up(scatter_row(add_up(grad_in), 0))
    bias_terms = jnp.sum(place_rows(row_blocks(bias_terms), 0), axis=0)
    grad_in_bias = jnp.where(at_home, bias_terms, other(bias_terms))
    grad_down, grad_up, grad_out = (add_up(v) for v in (grad_down, grad_up, grad_out))

    sums = jnp.split(sums, [model * k for k in range(1, 7)])
    grad_up_bias = lax.dynamic_index_in_dim(
        sums[6].reshape(2, n_col, half), c, 1, keepdims=False
    ).reshape(2 * half)

    grad_down = join(grad_down, 0)
    grad_up = join(grad_up.T, 1)
    grad_out = join(grad_out, 0)
    grad_in = join(grad_in, 0)
    grad_in = grad_in.reshape(part, groups, 3, per_group, HD).transpose(0, 1, 3, 2, 4)
    grad_in = grad_in.reshape(part, 3 * width)
    return (
        output,
        grad_tokens,
        grad_in,
        grad_in_bias,
        grad_out,
        sums[0],
        sums[1],
        sums[2],
        grad_up,
        grad_up_bias,
        grad_down,
        sums[3],
        sums[4],
        sums[5],
    )


def solution(mesh):
    return jax.shard_map(
        partial(on_device, tuple(mesh.shape[name] for name in ALL)),
        mesh=mesh,
        in_specs=(
            P(("dp", "row", "col"), None),
            P(("dp", "row"), None),
            P("row", "col"),
            P("col"),
            P("col", "row"),
            P(),
            P(),
            P(),
            P("row", "col"),
            P("col"),
            P("col", "row"),
            P(),
            P(),
            P(),
            P(("dp", "row", "col"), None),
        ),
        out_specs=(
            P(("dp", "row", "col"), None),
            P(("dp", "row", "col"), None),
            P("row", "col"),
            P("col"),
            P("col", "row"),
            P(),
            P(),
            P(),
            P("row", "col"),
            P("col"),
            P("col", "row"),
            P(),
            P(),
            P(),
        ),
        check_vma=False,
    )
```

```python
from functools import partial
import math

import jax
import jax.numpy as jnp
from jax import lax
from jax.experimental import pallas as pl
from jax.experimental.pallas import tpu as pltpu
from jax.sharding import PartitionSpec as P

HD = 64
NORM_EPSILON = 1e-12
ALL = ("dp", "row", "col")
BF = jnp.bfloat16
F32 = jnp.float32
HIDDEN_SCORE = -1e30
SCALE = HD ** (-0.5)
EXP2_SCALE = SCALE * math.log2(math.e)


class Grid:
    def __init__(self, dp, row, outer, inner):
        self.shape = (dp, row, outer, inner)

    def pairs(self, target):
        n_d, n_r, n_o, n_i = self.shape

        def flat(d, r, o, i):
            return ((d * n_r + r) * n_o + o) * n_i + i

        result = []
        for d in range(n_d):
            for r in range(n_r):
                for o in range(n_o):
                    for i in range(n_i):
                        there = target(d, r, o, i)
                        if there is not None:
                            result.append((flat(d, r, o, i), flat(*there)))
        return result

    def shift(self, value, axis, by):
        size = self.shape[axis]

        def target(*at):
            at = list(at)
            at[axis] = (at[axis] + by) % size
            return tuple(at)

        return lax.ppermute(value, ALL, self.pairs(target))

    def flip(self, value, axis, bit):
        def target(*at):
            at = list(at)
            at[axis] = at[axis] ^ bit
            return tuple(at)

        return lax.ppermute(value, ALL, self.pairs(target))

    def total(self, value, axes):
        for axis in axes:
            size = self.shape[axis]
            bit = 1
            while bit < size:
                value = value + self.flip(value, axis, bit)
                bit *= 2
        return value


def dot(left, right):
    return jnp.dot(left, right, preferred_element_type=F32)


def dot_t(left, right):
    return lax.dot_general(left, right, (((1,), (1,)), ((), ())), preferred_element_type=F32)


def t_dot(left, right):
    return lax.dot_general(left, right, (((0,), (0,)), ((), ())), preferred_element_type=F32)


def after(value, *earlier):
    return lax.optimization_barrier((value, *earlier))[0]


def norm_forward(hidden, gain, shift):
    row_mean = jnp.mean(hidden, axis=1, keepdims=True)
    variance = jnp.mean(hidden * hidden, axis=1, keepdims=True) - row_mean * row_mean
    inverse = lax.rsqrt(variance + NORM_EPSILON)
    normed = (hidden - row_mean) * inverse
    return (normed * gain + shift, normed, inverse)


def norm_backward(grad_after, normed, inverse, gain):
    grad_normed = grad_after * gain
    mean_one = jnp.mean(grad_normed, axis=1, keepdims=True)
    mean_two = jnp.mean(grad_normed * normed, axis=1, keepdims=True)
    return inverse * (grad_normed - mean_one - normed * mean_two)


def head_groups(width):
    columns = min(128, width)
    return columns, columns // HD, width // columns


def attend_forward_kernel(width, block, qkv, ids_row, ids_col, *rest):
    out, logs = rest[-2:]
    length = qkv.shape[1]
    columns, per_group, groups = head_groups(width)
    lane = lax.broadcasted_iota(jnp.int32, (block, columns), 1) // HD
    log_lane = lax.broadcasted_iota(jnp.int32, (block, 128), 1)

    @pl.loop(0, length // block)
    def _(step):
        rows = pl.ds(pl.multiple_of(step * block, block), block)
        same = ids_col[0, rows, :] == ids_row[0]
        row_logs = jnp.zeros((block, 128), F32)
        for group in range(groups):
            first = 3 * group * columns
            queries = qkv[0, rows, first : first + columns]
            keys = qkv[0, :, first + columns : first + 2 * columns]
            values = qkv[0, :, first + 2 * columns : first + 3 * columns]
            result = None
            for head in range(per_group):
                masked = jnp.where(lane == head, queries, jnp.zeros_like(queries))
                scores = jnp.where(same, dot_t(masked, keys), HIDDEN_SCORE)
                top = jnp.max(scores, axis=1, keepdims=True)
                terms = jnp.exp2((scores - top) * EXP2_SCALE)
                total = jnp.sum(terms, axis=1, keepdims=True)
                part = dot(terms.astype(BF), values) / total
                result = part if result is None else jnp.where(lane == head, part, result)
                log = top * EXP2_SCALE + jnp.log(total) * math.log2(math.e)
                row_logs = jnp.where(log_lane == group * per_group + head, log, row_logs)
            out[0, rows, group * columns : (group + 1) * columns] = result.astype(BF)
        logs[0, :, rows] = row_logs.T[: logs.shape[1]]


def attend_backward_kernel(
    width, block, group, ranges, qkv, grads, attended, logs, ids_row, ids_col, *rest
):
    out, query_total, key_total, value_total = rest[-4:]
    length = qkv.shape[1]
    columns, per_group, groups = head_groups(width)
    blocks = length // block
    sequence = pl.program_id(0)
    lane = lax.broadcasted_iota(jnp.int32, (block, columns), 1) // HD
    pick = lax.broadcasted_iota(jnp.int32, (8, columns), 0)
    pick = (pick == lax.broadcasted_iota(jnp.int32, (8, columns), 1) // HD).astype(F32)
    def low(at):
        return ranges[sequence, 0, at]

    def high(at):
        return ranges[sequence, 1, at]

    first, outer_first = 3 * group * columns, group * columns
    for total in (query_total, key_total, value_total):
        total[...] = jnp.zeros_like(total)

    @pl.loop(0, blocks)
    def _(step):
        rows = pl.ds(pl.multiple_of(step * block, block), block)
        row_ids = ids_row[0, :, rows]
        queries = qkv[0, rows, first : first + columns]
        tops = grads[0, rows, outer_first : outer_first + columns]
        results = attended[0, rows, outer_first : outer_first + columns]
        inner = lax.dot_general(
            pick,
            tops.astype(F32) * results.astype(F32),
            (((1,), (1,)), ((), ())),
            precision=lax.Precision.HIGHEST,
            preferred_element_type=F32,
        )
        nothing = jnp.zeros_like(queries)
        head_queries = [jnp.where(lane == head, queries, nothing) for head in range(per_group)]
        head_grads = [jnp.where(lane == head, tops, nothing) for head in range(per_group)]
        head_logs = [
            logs[0, pl.ds(group * per_group + head, 1), rows] for head in range(per_group)
        ]

        @pl.loop(0, blocks)
        def _(key_step):
            @pl.when((low(step) <= high(key_step)) & (low(key_step) <= high(step)))
            def _():
                at = pl.ds(pl.multiple_of(key_step * block, block), block)
                keys = qkv[0, at, first + columns : first + 2 * columns]
                values = qkv[0, at, first + 2 * columns : first + 3 * columns]
                same = ids_col[0, at, :] == row_ids
                query_part, key_part, value_part = 0.0, 0.0, 0.0
                for head in range(per_group):
                    scores = dot_t(keys, head_queries[head]) * EXP2_SCALE - head_logs[head]
                    probs = jnp.exp2(jnp.where(same, scores, HIDDEN_SCORE))
                    prob_grads = dot_t(values, head_grads[head])
                    score_grads = (probs * (prob_grads - inner[head : head + 1])).astype(BF)
                    head_keys = jnp.where(lane == head, keys, jnp.zeros_like(keys))
                    value_part += dot(probs.astype(BF), head_grads[head])
                    key_part += dot(score_grads, head_queries[head])
                    query_part += t_dot(score_grads, head_keys)
                value_total[at, :] += value_part
                key_total[at, :] += key_part
                query_total[rows, :] += query_part

    out[0, :, :columns] = (query_total[...] * SCALE).astype(BF)
    out[0, :, columns : 2 * columns] = (key_total[...] * SCALE).astype(BF)
    out[0, :, 2 * columns :] = value_total[...].astype(BF)


def whole_block(shape):
    return pl.BlockSpec((1,) + shape[1:], lambda s, *_: (s, 0, 0))


SMALL_COST = pl.CostEstimate(flops=1024, bytes_accessed=1024, transcendentals=0)


def attend_forward(qkv, ids, earlier):
    count, length, columns = qkv.shape
    width = columns // 3
    ids_row, ids_col = ids[:, None, :], ids[:, :, None]
    log_rows = -(-width // HD // 8) * 8
    return pl.pallas_call(
        partial(attend_forward_kernel, width, min(256, length)),
        grid=(count,),
        in_specs=[whole_block(v.shape) for v in (qkv, ids_row, ids_col)]
        + [pl.BlockSpec(memory_space=pl.ANY)] * len(earlier),
        out_specs=[
            whole_block((count, length, width)),
            whole_block((count, log_rows, length)),
        ],
        out_shape=[
            jax.ShapeDtypeStruct((count, length, width), BF),
            jax.ShapeDtypeStruct((count, log_rows, length), F32),
        ],
        compiler_params=pltpu.CompilerParams(vmem_limit_bytes=48 * 1024 * 1024),
        cost_estimate=SMALL_COST,
    )(qkv, ids_row, ids_col, *earlier)


def attend_backward(qkv, grads, attended, logs, ids, group, others):
    count, length, columns = qkv.shape
    width = columns // 3
    wide = head_groups(width)[0]
    block = min(256, length)
    ids_row, ids_col = ids[:, None, :], ids[:, :, None]
    blocked = ids.reshape(count, length // block, block)
    ranges = jnp.stack([jnp.min(blocked, axis=2), jnp.max(blocked, axis=2)], axis=1)
    operands = (qkv, grads, attended, logs, ids_row, ids_col)
    kept = () if others is None else (others,)
    return pl.pallas_call(
        partial(attend_backward_kernel, width, block, group),
        grid_spec=pltpu.PrefetchScalarGridSpec(
            num_scalar_prefetch=1,
            grid=(count,),
            in_specs=[whole_block(v.shape) for v in operands]
            + [pl.BlockSpec(memory_space=pl.ANY)] * len(kept),
            out_specs=pl.BlockSpec((1, length, 3 * wide), lambda s, *_: (s, 0, group)),
            scratch_shapes=[pltpu.VMEM((length, wide), F32)] * 3,
        ),
        out_shape=jax.ShapeDtypeStruct(qkv.shape, BF),
        input_output_aliases={1 + len(operands): 0} if kept else {},
        compiler_params=pltpu.CompilerParams(vmem_limit_bytes=48 * 1024 * 1024),
        cost_estimate=SMALL_COST,
    )(ranges, *operands, *kept)


D_AX, R_AX, O_AX, I_AX = 0, 1, 2, 3


def gelu_pair(value):
    cdf = 0.5 * (1.0 + lax.erf(value * (0.5**0.5)))
    density = jnp.exp(-0.5 * value * value) * (1.0 / math.sqrt(2.0 * math.pi))
    return value * cdf, cdf + value * density


def on_device(
    sizes,
    tokens,
    segment_ids,
    in_weight,
    in_bias,
    out_weight,
    out_bias,
    gain_one,
    shift_one,
    up_weight,
    up_bias,
    down_weight,
    down_bias,
    gain_two,
    shift_two,
    cotangent,
):
    n_dp, n_row, n_col = sizes
    rows_here, model = tokens.shape
    n_outer, length = segment_ids.shape
    n_inner = length // rows_here
    assert n_dp == 2 and n_outer == 2 and n_outer * n_inner == n_col
    net = Grid(n_dp, n_row, n_outer, n_inner)
    d, r, c = (lax.axis_index(name) for name in ALL)
    o, i = c // n_inner, c % n_inner
    at_home = o == d
    width = in_weight.shape[1] // 3
    heads = width // HD
    wide, per_group, groups = head_groups(width)
    part = model // n_row
    units = up_weight.shape[1]
    half = units // 2

    def place(k):
        return lax.rem(r - k + n_row, n_row)

    def other(value):
        return net.shift(value, D_AX, 1)

    def across_outer(value):
        return net.shift(value, O_AX, 1)

    def in_order(mine, theirs, axis):
        first = jnp.where(d == 0, mine, theirs)
        second = jnp.where(d == 0, theirs, mine)
        return jnp.concatenate([first, second], axis=axis)

    def row_blocks(value):
        return [value] + [net.shift(value, R_AX, k) for k in range(1, n_row)]

    def place_rows(blocks, axis):
        shape = list(blocks[0].shape)
        step = shape[axis]
        shape[axis] = step * n_row
        result = jnp.zeros(shape, blocks[0].dtype)
        for k, block in enumerate(blocks):
            result = lax.dynamic_update_slice_in_dim(result, block, place(k) * step, axis)
        return result

    def scatter_row(value, axis):
        step = value.shape[axis] // n_row
        terms = [lax.dynamic_slice_in_dim(value, r * step, step, axis).astype(F32)]
        for k in range(1, n_row):
            block = lax.dynamic_slice_in_dim(value, place(k) * step, step, axis)
            terms.append(net.shift(block.astype(BF), R_AX, -k))
        return terms

    def row_parts(value, axis):
        step = value.shape[axis] // n_row
        own = lax.dynamic_slice_in_dim(value, r * step, step, axis)
        return own, [
            lax.dynamic_slice_in_dim(value, place(k) * step, step, axis).astype(BF)
            for k in range(1, n_row)
        ]

    def add_up(terms):
        return sum(v.astype(F32) for v in terms)

    def gather_near(value):
        near = [value] + [net.shift(value, I_AX, k) for k in range(1, n_inner)]
        return near + [across_outer(value)]

    def gather_far(near, outer_share):
        near, away = near[:n_inner], near[n_inner]
        cut = int(away.shape[0] * outer_share)
        far = []
        for k in range(1, n_inner):
            pieces = [across_outer(near[k][:cut])]
            if cut < away.shape[0]:
                pieces.append(net.shift(away[cut:], I_AX, k))
            far.append(jnp.concatenate(pieces, axis=0))
        return near + [away] + far

    def scatter_far(blocks):
        return blocks[: n_inner + 1], [across_outer(v.astype(BF)) for v in blocks[n_inner + 1 :]]

    def scatter_near(parts, earlier=()):
        blocks, passed = parts
        terms = [blocks[0], across_outer(after(blocks[n_inner].astype(BF), *earlier))]
        for k in range(1, n_inner):
            sent = (blocks[k].astype(F32) + passed[k - 1].astype(F32)).astype(BF)
            terms.append(net.shift(after(sent, *earlier), I_AX, -k))
        return terms

    def exchange_blocks(value, away):
        keep = jnp.where(at_home, value, away)
        return keep, other(jnp.where(at_home, away, value))

    def return_blocks(mine, theirs):
        received = other(theirs).astype(F32)
        keep = jnp.where(at_home, mine, received)
        away = jnp.where(at_home, received, mine)
        return keep, away.astype(BF)

    def join(value, axis):
        return in_order(value, other(value), axis)

    small = jnp.concatenate([in_bias, up_bias])
    small_near = gather_near(small)
    small_blocks = gather_far(small_near, 1.0)
    in_mine = in_weight.reshape(2, part // 2, groups, per_group, 3, HD)
    in_mine = lax.dynamic_index_in_dim(in_mine, d, 0, keepdims=False)
    in_mine = in_mine.transpose(0, 1, 3, 2, 4).reshape(part // 2, 3 * width)
    in_row = place_rows(row_blocks(in_mine), 0)
    token_parts = [tokens]
    for k in range(1, n_inner):
        token_parts.append(net.shift(after(tokens, *small_near), I_AX, k))
    in_row, small_blocks = lax.optimization_barrier((in_row, small_blocks))
    up_mine = lax.dynamic_slice_in_dim(after(up_weight, in_row), d * half, half, 1)
    up_row = row_blocks(up_mine)
    in_away = across_outer(in_row)
    in_row, in_away, token_parts, up_row, out_weight = lax.optimization_barrier(
        (in_row, in_away, token_parts, up_row, out_weight)
    )
    up_row = place_rows(up_row, 0)
    up_near = gather_near(up_row)
    in_halves = exchange_blocks(in_row, in_away)
    bias_rows = jnp.where(
        at_home, small_blocks[0][: 2 * width], small_blocks[n_inner][: 2 * width]
    ).reshape(groups, per_group, 2, HD)
    in_bias_row = jnp.stack(
        [bias_rows[:, :, 0], jnp.zeros_like(bias_rows[:, :, 0]), bias_rows[:, :, 1]], axis=1
    ).reshape(3 * width)
    up_bias_blocks = [
        lax.dynamic_slice_in_dim(v[2 * width :], d * half, half, 0) for v in small_blocks
    ]
    in_full = in_order(
        *(v.reshape(n_row, 1, part // 2, 3 * width) for v in in_halves), 1
    ).reshape(model, 3 * width)
    out_mine = lax.dynamic_slice_in_dim(out_weight, d * (width // 2), width // 2, 0)
    out_row = place_rows(row_blocks(out_mine), 1)
    out_away = across_outer(out_row)
    def spread(parts):
        return jnp.concatenate(parts, axis=0), jnp.concatenate([other(v) for v in parts], axis=0)

    def collect_here(product):
        arrived = [other(product(1, k).astype(BF)) for k in range(n_inner)]
        sums = [product(0, k) + arrived[k].astype(F32) for k in range(n_inner)]
        return sums[0], [v.astype(BF) for v in sums[1:]]

    def collect(own, sent):
        for k, value in enumerate(sent):
            own = own + net.shift(value, I_AX, -k - 1).astype(F32)
        return own

    def part_rows(k):
        return slice(k * rows_here, (k + 1) * rows_here)

    own_ids = lax.dynamic_index_in_dim(segment_ids, o, 0, keepdims=False)
    own_ids = jnp.concatenate(
        [
            lax.dynamic_slice_in_dim(
                own_ids, lax.rem(i - k + n_inner, n_inner) * rows_here, rows_here, 0
            )
            for k in range(n_inner)
        ]
    )
    ids = jnp.stack([own_ids, other(own_ids)])

    token_full = jnp.concatenate(spread(token_parts), axis=0)
    projected = (dot(token_full, in_full) + in_bias_row).astype(BF)
    projected = projected.reshape(2, length, 3 * width)
    down_mine = lax.dynamic_slice_in_dim(down_weight, d * half, half, 0)
    down_row = place_rows(row_blocks(after(down_mine, projected)), 1)
    attended, logs = attend_forward(projected, ids, (up_row,))
    attended, up_near, down_row, out_away = lax.optimization_barrier(
        (attended, up_near, down_row, out_away)
    )
    out_full = in_order(*exchange_blocks(out_row, out_away), 0)
    down_away = across_outer(down_row)
    branch = collect(*collect_here(lambda seq, k: dot(attended[seq, part_rows(k)], out_full)))
    token_late = after(token_full, attended)
    step = part // 2
    halves_of = [
        jnp.concatenate(
            [token_late[:, k * step : (k + 1) * step] for k in range(at, 2 * n_row, 2)], axis=1
        )
        for at in range(2)
    ]
    token_halves = (
        jnp.where(d == 0, halves_of[0], halves_of[1]),
        jnp.where(d == 0, halves_of[1], halves_of[0]),
    )
    branch, down_away, token_halves = lax.optimization_barrier((branch, down_away, token_halves))
    up_blocks = gather_far(up_near, 1.0)
    down_near = gather_near(after(down_row, branch))[:n_inner] + [down_away]
    down_blocks = gather_far(down_near, 0.5)

    def lay_out(blocks, axis):
        shape = list(blocks[0].shape)
        step = shape[axis]
        shape[axis] = step * len(blocks)
        result = jnp.zeros(shape, blocks[0].dtype)
        for k, block in enumerate(blocks):
            result = lax.dynamic_update_slice_in_dim(result, block, k * step, axis)
        return result

    up_full, down_full = lay_out(up_blocks, 1), lay_out(down_blocks, 0)
    up_bias_row = jnp.concatenate(up_bias_blocks)
    residual_one = tokens.astype(F32) + (branch + out_bias)
    normed_one, unit_one, inverse_one = norm_forward(residual_one, gain_one, shift_one)

    def both(value):
        return jnp.concatenate([value, other(value)], axis=0)

    def across(value, weights_of):
        away = other(weights_of(value[rows_here:]).astype(BF))
        return weights_of(value[:rows_here]) + away.astype(F32)

    mid = both(normed_one.astype(BF))
    hidden, slope = lax.optimization_barrier(
        [v.astype(BF) for v in gelu_pair(dot(mid, up_full) + up_bias_row)]
    )
    residual_two = normed_one + (across(hidden, lambda v: dot(v, down_full)) + down_bias)
    normed_two, unit_two, inverse_two = norm_forward(residual_two, gain_two, shift_two)
    output = normed_two.astype(BF)

    grad_top = cotangent.astype(F32)
    grad_gain_two = jnp.sum(grad_top * unit_two, axis=0)
    grad_shift_two = jnp.sum(grad_top, axis=0)
    grad_two = norm_backward(grad_top, unit_two, inverse_two, gain_two)
    grad_two_low = grad_two.astype(BF)
    grad_down_bias = jnp.sum(grad_two_low.astype(F32), axis=0)
    grad_two_both = both(grad_two_low)

    def unit_blocks(value):
        return [value[k * half : (k + 1) * half] for k in range(n_col)]

    grad_down = scatter_far(unit_blocks(t_dot(hidden, grad_two_both).astype(BF)))
    grad_pre = (dot_t(grad_two_both, down_full) * slope.astype(F32)).astype(BF)
    grad_one = grad_two + across(grad_pre, lambda v: dot_t(v, up_full))
    unit_sums = unit_blocks(jnp.sum(grad_pre.astype(F32), axis=0))
    grad_up_bias = jnp.zeros((2, n_outer, n_inner, half), F32)
    for k in range(n_col):
        there_o = lax.rem(o - k // n_inner + n_outer, n_outer)
        there_i = lax.rem(i - k % n_inner + n_inner, n_inner)
        grad_up_bias = lax.dynamic_update_slice(
            grad_up_bias,
            unit_sums[k][None, None, None],
            (d, there_o, there_i, 0),
        )

    grad_gain_one = jnp.sum(grad_one * unit_one, axis=0)
    grad_shift_one = jnp.sum(grad_one, axis=0)
    grad_first = norm_backward(grad_one, unit_one, inverse_one, gain_one)
    grad_first_low = grad_first.astype(BF)
    grad_out_bias = jnp.sum(grad_first_low.astype(F32), axis=0)

    flat = [
        grad_out_bias,
        grad_gain_one,
        grad_shift_one,
        grad_down_bias,
        grad_gain_two,
        grad_shift_two,
        grad_up_bias.reshape(-1),
    ]
    first_parts = [grad_first_low]
    first_parts += [net.shift(grad_first_low, I_AX, k) for k in range(1, n_inner)]
    mid_late = after(mid, grad_first_low)
    grad_up = scatter_far(unit_blocks(t_dot(grad_pre, mid_late).astype(BF)))
    grad_first_both = spread(first_parts)
    grad_down = scatter_near(grad_down, first_parts)
    grad_attended = jnp.stack([dot_t(v, out_full).astype(BF) for v in grad_first_both])

    def halves(value, axis):
        step = value.shape[axis] // 2
        return [
            lax.dynamic_slice_in_dim(value, at * step, step, axis) for at in (d, 1 - d)
        ]

    out_mine, out_theirs = (
        [sum(t_dot(v, w) for v, w in zip(pair, grad_first_both)) for pair in
         zip(*(halves(v, 1) for v in attended))]
    )
    grad_out, out_away = return_blocks(out_mine, out_theirs.astype(BF))
    grad_out = [grad_out, across_outer(out_away)]
    projected_grads = None
    for g in range(groups):
        if g == groups - 1:
            grad_attended, grad_down, grad_up, projected_grads = lax.optimization_barrier(
                (grad_attended, grad_down, grad_up, projected_grads)
            )
            grad_up = scatter_near(grad_up)
            grad_down = scatter_row(add_up(grad_down), 1)
        projected_grads = attend_backward(
            projected, grad_attended, attended, logs, ids, g, projected_grads
        )
    projected_grads, grad_up, grad_down, grad_out = lax.optimization_barrier(
        (projected_grads, grad_up, grad_down, grad_out)
    )
    grad_out = row_parts(add_up(grad_out), 1)
    sent = collect_here(lambda seq, k: dot_t(projected_grads[seq, part_rows(k)], in_full))
    in_mine, in_theirs = (
        sum(t_dot(v[k * length : (k + 1) * length], projected_grads[k]) for k in range(2))
        for v in token_halves
    )
    grad_in, in_away = return_blocks(in_mine, in_theirs.astype(BF))
    grad_up = row_parts(add_up(grad_up), 1)
    sent, grad_in, in_away, grad_up, grad_out, projected_grads = lax.optimization_barrier(
        (sent, grad_in, in_away, grad_up, grad_out, projected_grads)
    )
    grad_tokens = grad_first + collect(*sent)
    grad_in = [grad_in, across_outer(in_away)]
    grad_up, grad_out = (
        [own] + [net.shift(v, R_AX, -k - 1) for k, v in enumerate(parts)]
        for own, parts in (grad_up, grad_out)
    )
    bias_terms = jnp.sum(projected_grads.astype(F32), axis=(0, 1))
    bias_terms = bias_terms.reshape(groups, 3, per_group, HD)
    bias_terms = jnp.stack([bias_terms[:, 0], bias_terms[:, 2]], axis=2).reshape(1, 2 * width)
    bias_terms = lax.dynamic_update_slice_in_dim(
        jnp.zeros((n_col, 2 * width), F32), bias_terms, d * n_inner + i, 0
    )
    grad_up, grad_tokens, grad_in = lax.optimization_barrier((grad_up, grad_tokens, grad_in))
    flat = jnp.concatenate(flat + [bias_terms.reshape(-1)]).reshape(-1, 128)
    flat = after(flat, *grad_in)
    sums = net.total(flat, (R_AX, O_AX, I_AX, D_AX)).reshape(-1)
    grad_in = add_up(scatter_row(add_up(grad_in), 0))
    grad_down, grad_up, grad_out = (add_up(v) for v in (grad_down, grad_up, grad_out))

    sums = jnp.split(sums, [model * k for k in range(1, 7)] + [6 * model + 2 * n_col * half])
    grad_in_bias = lax.dynamic_index_in_dim(
        sums[7].reshape(n_col, 2 * width), c, 0, keepdims=False
    )
    grad_up_bias = lax.dynamic_index_in_dim(
        sums[6].reshape(2, n_col, half), c, 1, keepdims=False
    ).reshape(2 * half)

    grad_down = join(grad_down, 0)
    grad_up = join(grad_up.T, 1)
    grad_out = join(grad_out, 0)
    grad_in = join(grad_in, 0)
    grad_in = grad_in.reshape(part, groups, 3, per_group, HD).transpose(0, 1, 3, 2, 4)
    grad_in = grad_in.reshape(part, 3 * width)
    return (
        output,
        grad_tokens,
        grad_in,
        grad_in_bias,
        grad_out,
        sums[0],
        sums[1],
        sums[2],
        grad_up,
        grad_up_bias,
        grad_down,
        sums[3],
        sums[4],
        sums[5],
    )


def solution(mesh):
    return jax.shard_map(
        partial(on_device, tuple(mesh.shape[name] for name in ALL)),
        mesh=mesh,
        in_specs=(
            P(("dp", "row", "col"), None),
            P(("dp", "row"), None),
            P("row", "col"),
            P("col"),
            P("col", "row"),
            P(),
            P(),
            P(),
            P("row", "col"),
            P("col"),
            P("col", "row"),
            P(),
            P(),
            P(),
            P(("dp", "row", "col"), None),
        ),
        out_specs=(
            P(("dp", "row", "col"), None),
            P(("dp", "row", "col"), None),
            P("row", "col"),
            P("col"),
            P("col", "row"),
            P(),
            P(),
            P(),
            P("row", "col"),
            P("col"),
            P("col", "row"),
            P(),
            P(),
            P(),
        ),
        check_vma=False,
    )
```

```python
from functools import partial
import math

import jax
import jax.numpy as jnp
from jax import lax
from jax.experimental import pallas as pl
from jax.experimental.pallas import tpu as pltpu
from jax.sharding import PartitionSpec as P

HD = 64
NORM_EPSILON = 1e-12
ALL = ("dp", "row", "col")
BF = jnp.bfloat16
F32 = jnp.float32
HIDDEN_SCORE = -1e30
SCALE = HD ** (-0.5)
EXP2_SCALE = SCALE * math.log2(math.e)


class Grid:
    def __init__(self, dp, row, outer, inner):
        self.shape = (dp, row, outer, inner)

    def pairs(self, target):
        n_d, n_r, n_o, n_i = self.shape

        def flat(d, r, o, i):
            return ((d * n_r + r) * n_o + o) * n_i + i

        result = []
        for d in range(n_d):
            for r in range(n_r):
                for o in range(n_o):
                    for i in range(n_i):
                        there = target(d, r, o, i)
                        if there is not None:
                            result.append((flat(d, r, o, i), flat(*there)))
        return result

    def shift(self, value, axis, by):
        size = self.shape[axis]

        def target(*at):
            at = list(at)
            at[axis] = (at[axis] + by) % size
            return tuple(at)

        return lax.ppermute(value, ALL, self.pairs(target))

    def flip(self, value, axis, bit):
        def target(*at):
            at = list(at)
            at[axis] = at[axis] ^ bit
            return tuple(at)

        return lax.ppermute(value, ALL, self.pairs(target))

    def total(self, value, axes):
        for axis in axes:
            size = self.shape[axis]
            bit = 1
            while bit < size:
                value = value + self.flip(value, axis, bit)
                bit *= 2
        return value


def dot(left, right):
    return jnp.dot(left, right, preferred_element_type=F32)


def dot_t(left, right):
    return lax.dot_general(left, right, (((1,), (1,)), ((), ())), preferred_element_type=F32)


def t_dot(left, right):
    return lax.dot_general(left, right, (((0,), (0,)), ((), ())), preferred_element_type=F32)


def after(value, *earlier):
    return lax.optimization_barrier((value, *earlier))[0]


def norm_forward(hidden, gain, shift):
    row_mean = jnp.mean(hidden, axis=1, keepdims=True)
    variance = jnp.mean(hidden * hidden, axis=1, keepdims=True) - row_mean * row_mean
    inverse = lax.rsqrt(variance + NORM_EPSILON)
    normed = (hidden - row_mean) * inverse
    return (normed * gain + shift, normed, inverse)


def norm_backward(grad_after, normed, inverse, gain):
    grad_normed = grad_after * gain
    mean_one = jnp.mean(grad_normed, axis=1, keepdims=True)
    mean_two = jnp.mean(grad_normed * normed, axis=1, keepdims=True)
    return inverse * (grad_normed - mean_one - normed * mean_two)


def head_groups(width):
    columns = min(128, width)
    return columns, columns // HD, width // columns


def attend_forward_kernel(width, block, qkv, ids_row, ids_col, *rest):
    out, logs = rest[-2:]
    length = qkv.shape[1]
    columns, per_group, groups = head_groups(width)
    lane = lax.broadcasted_iota(jnp.int32, (block, columns), 1) // HD
    log_lane = lax.broadcasted_iota(jnp.int32, (block, 128), 1)

    @pl.loop(0, length // block)
    def _(step):
        rows = pl.ds(pl.multiple_of(step * block, block), block)
        same = ids_col[0, rows, :] == ids_row[0]
        row_logs = jnp.zeros((block, 128), F32)
        for group in range(groups):
            first = 3 * group * columns
            queries = qkv[0, rows, first : first + columns]
            keys = qkv[0, :, first + columns : first + 2 * columns]
            values = qkv[0, :, first + 2 * columns : first + 3 * columns]
            result = None
            for head in range(per_group):
                masked = jnp.where(lane == head, queries, jnp.zeros_like(queries))
                scores = jnp.where(same, dot_t(masked, keys), HIDDEN_SCORE)
                top = jnp.max(scores, axis=1, keepdims=True)
                terms = jnp.exp2((scores - top) * EXP2_SCALE)
                total = jnp.sum(terms, axis=1, keepdims=True)
                part = dot(terms.astype(BF), values) / total
                result = part if result is None else jnp.where(lane == head, part, result)
                log = top * EXP2_SCALE + jnp.log(total) * math.log2(math.e)
                row_logs = jnp.where(log_lane == group * per_group + head, log, row_logs)
            out[0, rows, group * columns : (group + 1) * columns] = result.astype(BF)
        logs[0, :, rows] = row_logs.T[: logs.shape[1]]


def attend_backward_kernel(
    width, block, group, ranges, qkv, grads, attended, logs, ids_row, ids_col, *rest
):
    out, query_total, key_total, value_total = rest[-4:]
    length = qkv.shape[1]
    columns, per_group, groups = head_groups(width)
    blocks = length // block
    sequence = pl.program_id(0)
    lane = lax.broadcasted_iota(jnp.int32, (block, columns), 1) // HD
    pick = lax.broadcasted_iota(jnp.int32, (8, columns), 0)
    pick = (pick == lax.broadcasted_iota(jnp.int32, (8, columns), 1) // HD).astype(F32)
    def low(at):
        return ranges[sequence, 0, at]

    def high(at):
        return ranges[sequence, 1, at]

    first, outer_first = 3 * group * columns, group * columns
    for total in (query_total, key_total, value_total):
        total[...] = jnp.zeros_like(total)

    @pl.loop(0, blocks)
    def _(step):
        rows = pl.ds(pl.multiple_of(step * block, block), block)
        row_ids = ids_row[0, :, rows]
        queries = qkv[0, rows, first : first + columns]
        tops = grads[0, rows, outer_first : outer_first + columns]
        results = attended[0, rows, outer_first : outer_first + columns]
        inner = lax.dot_general(
            pick,
            tops.astype(F32) * results.astype(F32),
            (((1,), (1,)), ((), ())),
            precision=lax.Precision.HIGHEST,
            preferred_element_type=F32,
        )
        nothing = jnp.zeros_like(queries)
        head_queries = [jnp.where(lane == head, queries, nothing) for head in range(per_group)]
        head_grads = [jnp.where(lane == head, tops, nothing) for head in range(per_group)]
        head_logs = [
            logs[0, pl.ds(group * per_group + head, 1), rows] for head in range(per_group)
        ]

        @pl.loop(0, blocks)
        def _(key_step):
            @pl.when((low(step) <= high(key_step)) & (low(key_step) <= high(step)))
            def _():
                at = pl.ds(pl.multiple_of(key_step * block, block), block)
                keys = qkv[0, at, first + columns : first + 2 * columns]
                values = qkv[0, at, first + 2 * columns : first + 3 * columns]
                same = ids_col[0, at, :] == row_ids
                query_part, key_part, value_part = 0.0, 0.0, 0.0
                for head in range(per_group):
                    scores = dot_t(keys, head_queries[head]) * EXP2_SCALE - head_logs[head]
                    probs = jnp.exp2(jnp.where(same, scores, HIDDEN_SCORE))
                    prob_grads = dot_t(values, head_grads[head])
                    score_grads = (probs * (prob_grads - inner[head : head + 1])).astype(BF)
                    head_keys = jnp.where(lane == head, keys, jnp.zeros_like(keys))
                    value_part += dot(probs.astype(BF), head_grads[head])
                    key_part += dot(score_grads, head_queries[head])
                    query_part += t_dot(score_grads, head_keys)
                value_total[at, :] += value_part
                key_total[at, :] += key_part
                query_total[rows, :] += query_part

    out[0, :, :columns] = (query_total[...] * SCALE).astype(BF)
    out[0, :, columns : 2 * columns] = (key_total[...] * SCALE).astype(BF)
    out[0, :, 2 * columns :] = value_total[...].astype(BF)


def whole_block(shape):
    return pl.BlockSpec((1,) + shape[1:], lambda s, *_: (s, 0, 0))


SMALL_COST = pl.CostEstimate(flops=1024, bytes_accessed=1024, transcendentals=0)


def attend_forward(qkv, ids, earlier):
    count, length, columns = qkv.shape
    width = columns // 3
    ids_row, ids_col = ids[:, None, :], ids[:, :, None]
    log_rows = -(-width // HD // 8) * 8
    return pl.pallas_call(
        partial(attend_forward_kernel, width, min(512, length)),
        grid=(count,),
        in_specs=[whole_block(v.shape) for v in (qkv, ids_row, ids_col)]
        + [pl.BlockSpec(memory_space=pl.ANY)] * len(earlier),
        out_specs=[
            whole_block((count, length, width)),
            whole_block((count, log_rows, length)),
        ],
        out_shape=[
            jax.ShapeDtypeStruct((count, length, width), BF),
            jax.ShapeDtypeStruct((count, log_rows, length), F32),
        ],
        compiler_params=pltpu.CompilerParams(vmem_limit_bytes=48 * 1024 * 1024),
        cost_estimate=SMALL_COST,
    )(qkv, ids_row, ids_col, *earlier)


def attend_backward(qkv, grads, attended, logs, ids, group, others):
    count, length, columns = qkv.shape
    width = columns // 3
    wide = head_groups(width)[0]
    block = min(256, length)
    ids_row, ids_col = ids[:, None, :], ids[:, :, None]
    blocked = ids.reshape(count, length // block, block)
    ranges = jnp.stack([jnp.min(blocked, axis=2), jnp.max(blocked, axis=2)], axis=1)
    operands = (qkv, grads, attended, logs, ids_row, ids_col)
    kept = () if others is None else (others,)
    return pl.pallas_call(
        partial(attend_backward_kernel, width, block, group),
        grid_spec=pltpu.PrefetchScalarGridSpec(
            num_scalar_prefetch=1,
            grid=(count,),
            in_specs=[whole_block(v.shape) for v in operands]
            + [pl.BlockSpec(memory_space=pl.ANY)] * len(kept),
            out_specs=pl.BlockSpec((1, length, 3 * wide), lambda s, *_: (s, 0, group)),
            scratch_shapes=[pltpu.VMEM((length, wide), F32)] * 3,
        ),
        out_shape=jax.ShapeDtypeStruct(qkv.shape, BF),
        input_output_aliases={1 + len(operands): 0} if kept else {},
        compiler_params=pltpu.CompilerParams(vmem_limit_bytes=48 * 1024 * 1024),
        cost_estimate=SMALL_COST,
    )(ranges, *operands, *kept)


D_AX, R_AX, O_AX, I_AX = 0, 1, 2, 3


def gelu_pair(value):
    cdf = 0.5 * (1.0 + lax.erf(value * (0.5**0.5)))
    density = jnp.exp(-0.5 * value * value) * (1.0 / math.sqrt(2.0 * math.pi))
    return value * cdf, cdf + value * density


def on_device(
    sizes,
    tokens,
    segment_ids,
    in_weight,
    in_bias,
    out_weight,
    out_bias,
    gain_one,
    shift_one,
    up_weight,
    up_bias,
    down_weight,
    down_bias,
    gain_two,
    shift_two,
    cotangent,
):
    n_dp, n_row, n_col = sizes
    rows_here, model = tokens.shape
    n_outer, length = segment_ids.shape
    n_inner = length // rows_here
    assert n_dp == 2 and n_outer == 2 and n_outer * n_inner == n_col
    net = Grid(n_dp, n_row, n_outer, n_inner)
    d, r, c = (lax.axis_index(name) for name in ALL)
    o, i = c // n_inner, c % n_inner
    at_home = o == d
    width = in_weight.shape[1] // 3
    heads = width // HD
    wide, per_group, groups = head_groups(width)
    part = model // n_row
    units = up_weight.shape[1]
    half = units // 2

    def place(k):
        return lax.rem(r - k + n_row, n_row)

    def other(value):
        return net.shift(value, D_AX, 1)

    def across_outer(value):
        return net.shift(value, O_AX, 1)

    def in_order(mine, theirs, axis):
        first = jnp.where(d == 0, mine, theirs)
        second = jnp.where(d == 0, theirs, mine)
        return jnp.concatenate([first, second], axis=axis)

    def row_blocks(value):
        return [value] + [net.shift(value, R_AX, k) for k in range(1, n_row)]

    def place_rows(blocks, axis):
        shape = list(blocks[0].shape)
        step = shape[axis]
        shape[axis] = step * n_row
        result = jnp.zeros(shape, blocks[0].dtype)
        for k, block in enumerate(blocks):
            result = lax.dynamic_update_slice_in_dim(result, block, place(k) * step, axis)
        return result

    def scatter_row(value, axis):
        step = value.shape[axis] // n_row
        terms = [lax.dynamic_slice_in_dim(value, r * step, step, axis).astype(F32)]
        for k in range(1, n_row):
            block = lax.dynamic_slice_in_dim(value, place(k) * step, step, axis)
            terms.append(net.shift(block.astype(BF), R_AX, -k))
        return terms

    def row_parts(value, axis):
        step = value.shape[axis] // n_row
        own = lax.dynamic_slice_in_dim(value, r * step, step, axis)
        return own, [
            lax.dynamic_slice_in_dim(value, place(k) * step, step, axis).astype(BF)
            for k in range(1, n_row)
        ]

    def add_up(terms):
        return sum(v.astype(F32) for v in terms)

    def gather_near(value):
        near = [value] + [net.shift(value, I_AX, k) for k in range(1, n_inner)]
        return near + [across_outer(value)]

    def gather_far(near, outer_share):
        near, away = near[:n_inner], near[n_inner]
        cut = int(away.shape[0] * outer_share)
        far = []
        for k in range(1, n_inner):
            pieces = [across_outer(near[k][:cut])]
            if cut < away.shape[0]:
                pieces.append(net.shift(away[cut:], I_AX, k))
            far.append(jnp.concatenate(pieces, axis=0))
        return near + [away] + far

    def scatter_far(blocks):
        return blocks[: n_inner + 1], [across_outer(v.astype(BF)) for v in blocks[n_inner + 1 :]]

    def scatter_near(parts, earlier=()):
        blocks, passed = parts
        terms = [blocks[0], across_outer(after(blocks[n_inner].astype(BF), *earlier))]
        for k in range(1, n_inner):
            sent = (blocks[k].astype(F32) + passed[k - 1].astype(F32)).astype(BF)
            terms.append(net.shift(after(sent, *earlier), I_AX, -k))
        return terms

    def exchange_blocks(value, away):
        keep = jnp.where(at_home, value, away)
        return keep, other(jnp.where(at_home, away, value))

    def return_blocks(mine, theirs):
        received = other(theirs).astype(F32)
        keep = jnp.where(at_home, mine, received)
        away = jnp.where(at_home, received, mine)
        return keep, away.astype(BF)

    def join(value, axis):
        return in_order(value, other(value), axis)

    small = jnp.concatenate([in_bias, up_bias])
    small_near = gather_near(small)
    small_blocks = gather_far(small_near, 1.0)
    in_mine = in_weight.reshape(2, part // 2, groups, per_group, 3, HD)
    in_mine = lax.dynamic_index_in_dim(in_mine, d, 0, keepdims=False)
    in_mine = in_mine.transpose(0, 1, 3, 2, 4).reshape(part // 2, 3 * width)
    in_row = place_rows(row_blocks(in_mine), 0)
    token_parts = [tokens]
    for k in range(1, n_inner):
        token_parts.append(net.shift(after(tokens, *small_near), I_AX, k))
    in_row, small_blocks = lax.optimization_barrier((in_row, small_blocks))
    up_mine = lax.dynamic_slice_in_dim(after(up_weight, in_row), d * half, half, 1)
    up_row = row_blocks(up_mine)
    in_away = across_outer(in_row)
    in_row, in_away, token_parts, up_row, out_weight = lax.optimization_barrier(
        (in_row, in_away, token_parts, up_row, out_weight)
    )
    up_row = place_rows(up_row, 0)
    up_near = gather_near(up_row)
    in_halves = exchange_blocks(in_row, in_away)
    bias_rows = jnp.where(
        at_home, small_blocks[0][: 2 * width], small_blocks[n_inner][: 2 * width]
    ).reshape(groups, per_group, 2, HD)
    in_bias_row = jnp.stack(
        [bias_rows[:, :, 0], jnp.zeros_like(bias_rows[:, :, 0]), bias_rows[:, :, 1]], axis=1
    ).reshape(3 * width)
    up_bias_blocks = [
        lax.dynamic_slice_in_dim(v[2 * width :], d * half, half, 0) for v in small_blocks
    ]
    in_full = in_order(
        *(v.reshape(n_row, 1, part // 2, 3 * width) for v in in_halves), 1
    ).reshape(model, 3 * width)
    out_mine = lax.dynamic_slice_in_dim(out_weight, d * (width // 2), width // 2, 0)
    out_row = place_rows(row_blocks(out_mine), 1)
    out_away = across_outer(out_row)
    def spread(parts):
        return jnp.concatenate(parts, axis=0), jnp.concatenate([other(v) for v in parts], axis=0)

    def collect_here(product):
        arrived = [other(product(1, k).astype(BF)) for k in range(n_inner)]
        sums = [product(0, k) + arrived[k].astype(F32) for k in range(n_inner)]
        return sums[0], [v.astype(BF) for v in sums[1:]]

    def collect(own, sent):
        for k, value in enumerate(sent):
            own = own + net.shift(value, I_AX, -k - 1).astype(F32)
        return own

    def part_rows(k):
        return slice(k * rows_here, (k + 1) * rows_here)

    own_ids = lax.dynamic_index_in_dim(segment_ids, o, 0, keepdims=False)
    own_ids = jnp.concatenate(
        [
            lax.dynamic_slice_in_dim(
                own_ids, lax.rem(i - k + n_inner, n_inner) * rows_here, rows_here, 0
            )
            for k in range(n_inner)
        ]
    )
    ids = jnp.stack([own_ids, other(own_ids)])

    token_full = jnp.concatenate(spread(token_parts), axis=0)
    projected = (dot(token_full, in_full) + in_bias_row).astype(BF)
    projected = projected.reshape(2, length, 3 * width)
    down_mine = lax.dynamic_slice_in_dim(down_weight, d * half, half, 0)
    down_row = place_rows(row_blocks(after(down_mine, projected)), 1)
    attended, logs = attend_forward(projected, ids, (up_row,))
    attended, up_near, down_row, out_away = lax.optimization_barrier(
        (attended, up_near, down_row, out_away)
    )
    out_full = in_order(*exchange_blocks(out_row, out_away), 0)
    down_away = across_outer(down_row)
    branch = collect(*collect_here(lambda seq, k: dot(attended[seq, part_rows(k)], out_full)))
    token_late = after(token_full, attended)
    step = part // 2
    halves_of = [
        jnp.concatenate(
            [token_late[:, k * step : (k + 1) * step] for k in range(at, 2 * n_row, 2)], axis=1
        )
        for at in range(2)
    ]
    token_halves = (
        jnp.where(d == 0, halves_of[0], halves_of[1]),
        jnp.where(d == 0, halves_of[1], halves_of[0]),
    )
    branch, down_away, token_halves = lax.optimization_barrier((branch, down_away, token_halves))
    up_blocks = gather_far(up_near, 1.0)
    down_near = gather_near(after(down_row, branch))[:n_inner] + [down_away]
    down_blocks = gather_far(down_near, 0.5)

    def lay_out(blocks, axis):
        shape = list(blocks[0].shape)
        step = shape[axis]
        shape[axis] = step * len(blocks)
        result = jnp.zeros(shape, blocks[0].dtype)
        for k, block in enumerate(blocks):
            result = lax.dynamic_update_slice_in_dim(result, block, k * step, axis)
        return result

    up_full, down_full = lay_out(up_blocks, 1), lay_out(down_blocks, 0)
    up_bias_row = jnp.concatenate(up_bias_blocks)
    residual_one = tokens.astype(F32) + (branch + out_bias)
    normed_one, unit_one, inverse_one = norm_forward(residual_one, gain_one, shift_one)

    def both(value):
        return jnp.concatenate([value, other(value)], axis=0)

    def across(value, weights_of):
        away = other(weights_of(value[rows_here:]).astype(BF))
        return weights_of(value[:rows_here]) + away.astype(F32)

    mid = both(normed_one.astype(BF))
    hidden, slope = lax.optimization_barrier(
        [v.astype(BF) for v in gelu_pair(dot(mid, up_full) + up_bias_row)]
    )
    residual_two = normed_one + (across(hidden, lambda v: dot(v, down_full)) + down_bias)
    normed_two, unit_two, inverse_two = norm_forward(residual_two, gain_two, shift_two)
    output = normed_two.astype(BF)

    grad_top = cotangent.astype(F32)
    grad_gain_two = jnp.sum(grad_top * unit_two, axis=0)
    grad_shift_two = jnp.sum(grad_top, axis=0)
    grad_two = norm_backward(grad_top, unit_two, inverse_two, gain_two)
    grad_two_low = grad_two.astype(BF)
    grad_down_bias = jnp.sum(grad_two_low.astype(F32), axis=0)
    grad_two_both = both(grad_two_low)

    def unit_blocks(value):
        return [value[k * half : (k + 1) * half] for k in range(n_col)]

    grad_down = scatter_far(unit_blocks(t_dot(hidden, grad_two_both).astype(BF)))
    grad_pre = (dot_t(grad_two_both, down_full) * slope.astype(F32)).astype(BF)
    grad_one = grad_two + across(grad_pre, lambda v: dot_t(v, up_full))
    unit_sums = unit_blocks(jnp.sum(grad_pre.astype(F32), axis=0))
    grad_up_bias = jnp.zeros((2, n_outer, n_inner, half), F32)
    for k in range(n_col):
        there_o = lax.rem(o - k // n_inner + n_outer, n_outer)
        there_i = lax.rem(i - k % n_inner + n_inner, n_inner)
        grad_up_bias = lax.dynamic_update_slice(
            grad_up_bias,
            unit_sums[k][None, None, None],
            (d, there_o, there_i, 0),
        )

    grad_gain_one = jnp.sum(grad_one * unit_one, axis=0)
    grad_shift_one = jnp.sum(grad_one, axis=0)
    grad_first = norm_backward(grad_one, unit_one, inverse_one, gain_one)
    grad_first_low = grad_first.astype(BF)
    grad_out_bias = jnp.sum(grad_first_low.astype(F32), axis=0)

    flat = [
        grad_out_bias,
        grad_gain_one,
        grad_shift_one,
        grad_down_bias,
        grad_gain_two,
        grad_shift_two,
        grad_up_bias.reshape(-1),
    ]
    first_parts = [grad_first_low]
    first_parts += [net.shift(grad_first_low, I_AX, k) for k in range(1, n_inner)]
    mid_late = after(mid, grad_first_low)
    grad_up = scatter_far(unit_blocks(t_dot(grad_pre, mid_late).astype(BF)))
    grad_first_both = spread(first_parts)
    grad_down = scatter_near(grad_down, first_parts)
    grad_attended = jnp.stack([dot_t(v, out_full).astype(BF) for v in grad_first_both])

    def halves(value, axis):
        step = value.shape[axis] // 2
        return [
            lax.dynamic_slice_in_dim(value, at * step, step, axis) for at in (d, 1 - d)
        ]

    out_mine, out_theirs = (
        [sum(t_dot(v, w) for v, w in zip(pair, grad_first_both)) for pair in
         zip(*(halves(v, 1) for v in attended))]
    )
    grad_out, out_away = return_blocks(out_mine, out_theirs.astype(BF))
    grad_out = [grad_out, across_outer(out_away)]
    projected_grads = None
    for g in range(groups):
        if g == groups - 1:
            grad_attended, grad_down, grad_up, projected_grads = lax.optimization_barrier(
                (grad_attended, grad_down, grad_up, projected_grads)
            )
            grad_up = scatter_near(grad_up)
            grad_down = scatter_row(add_up(grad_down), 1)
        projected_grads = attend_backward(
            projected, grad_attended, attended, logs, ids, g, projected_grads
        )
    projected_grads, grad_up, grad_down, grad_out = lax.optimization_barrier(
        (projected_grads, grad_up, grad_down, grad_out)
    )
    grad_out = row_parts(add_up(grad_out), 1)
    sent = collect_here(lambda seq, k: dot_t(projected_grads[seq, part_rows(k)], in_full))
    in_mine, in_theirs = (
        sum(t_dot(v[k * length : (k + 1) * length], projected_grads[k]) for k in range(2))
        for v in token_halves
    )
    grad_in, in_away = return_blocks(in_mine, in_theirs.astype(BF))
    grad_up = row_parts(add_up(grad_up), 1)
    sent, grad_in, in_away, grad_up, grad_out, projected_grads = lax.optimization_barrier(
        (sent, grad_in, in_away, grad_up, grad_out, projected_grads)
    )
    grad_tokens = grad_first + collect(*sent)
    grad_in = [grad_in, across_outer(in_away)]
    grad_up, grad_out = (
        [own] + [net.shift(v, R_AX, -k - 1) for k, v in enumerate(parts)]
        for own, parts in (grad_up, grad_out)
    )
    bias_terms = jnp.sum(projected_grads.astype(F32), axis=(0, 1))
    bias_terms = bias_terms.reshape(groups, 3, per_group, HD)
    bias_terms = jnp.stack([bias_terms[:, 0], bias_terms[:, 2]], axis=2).reshape(1, 2 * width)
    bias_terms = lax.dynamic_update_slice_in_dim(
        jnp.zeros((n_col, 2 * width), F32), bias_terms, d * n_inner + i, 0
    )
    grad_up, grad_tokens, grad_in = lax.optimization_barrier((grad_up, grad_tokens, grad_in))
    flat = jnp.concatenate(flat + [bias_terms.reshape(-1)]).reshape(-1, 128)
    flat = after(flat, *grad_in)
    sums = net.total(flat, (R_AX, O_AX, I_AX, D_AX)).reshape(-1)
    grad_in = add_up(scatter_row(add_up(grad_in), 0))
    grad_down, grad_up, grad_out = (add_up(v) for v in (grad_down, grad_up, grad_out))

    sums = jnp.split(sums, [model * k for k in range(1, 7)] + [6 * model + 2 * n_col * half])
    grad_in_bias = lax.dynamic_index_in_dim(
        sums[7].reshape(n_col, 2 * width), c, 0, keepdims=False
    )
    grad_up_bias = lax.dynamic_index_in_dim(
        sums[6].reshape(2, n_col, half), c, 1, keepdims=False
    ).reshape(2 * half)

    grad_down = join(grad_down, 0)
    grad_up = join(grad_up.T, 1)
    grad_out = join(grad_out, 0)
    grad_in = join(grad_in, 0)
    grad_in = grad_in.reshape(part, groups, 3, per_group, HD).transpose(0, 1, 3, 2, 4)
    grad_in = grad_in.reshape(part, 3 * width)
    return (
        output,
        grad_tokens,
        grad_in,
        grad_in_bias,
        grad_out,
        sums[0],
        sums[1],
        sums[2],
        grad_up,
        grad_up_bias,
        grad_down,
        sums[3],
        sums[4],
        sums[5],
    )


def solution(mesh):
    return jax.shard_map(
        partial(on_device, tuple(mesh.shape[name] for name in ALL)),
        mesh=mesh,
        in_specs=(
            P(("dp", "row", "col"), None),
            P(("dp", "row"), None),
            P("row", "col"),
            P("col"),
            P("col", "row"),
            P(),
            P(),
            P(),
            P("row", "col"),
            P("col"),
            P("col", "row"),
            P(),
            P(),
            P(),
            P(("dp", "row", "col"), None),
        ),
        out_specs=(
            P(("dp", "row", "col"), None),
            P(("dp", "row", "col"), None),
            P("row", "col"),
            P("col"),
            P("col", "row"),
            P(),
            P(),
            P(),
            P("row", "col"),
            P("col"),
            P("col", "row"),
            P(),
            P(),
            P(),
        ),
        check_vma=False,
    )
```
